128 devices in a mesh: lat: 4 (over y_hi, core), lon: 32 (over y_lo, z, x).
Axes of the slice: x: 4, y: 4 (y_hi: 2, y_lo: 2; y = y_hi * 2 + y_lo), z: 4, core: 2. Of those that a mesh axis runs over, the one named last changes fastest.
Arguments:
- observations: bfloat16 [16384, 32, 256], P(('lat', 'lon')), may hold values from -6 to 6
- slot_cells: int32 [16384, 32], P(('lat', 'lon')), may hold values from 0 to 4095
- slot_counts: int32 [16384], P(('lat', 'lon')), may hold values from 4 to 32, as said below
- conv_in: bfloat16 [3, 3, 256, 512], replicated, may hold values from -0.125 to 0.125
- conv_density: float32 [3, 3, 512], replicated, may hold values from -3.5 to 3.5
- bias_in: float32 [512], replicated, may hold values from -3 to 3
- conv_mid: bfloat16 [3, 3, 512, 512], replicated, may hold values from -0.09375 to 0.09375
- bias_mid: float32 [512], replicated, may hold values from -3 to 3
Outputs:
- encoded: bfloat16 [32, 1024, 512], P('lat', 'lon')
The draws below stay inside these ranges and needn't reach their ends.
Inputs may be any that keep to these rules, and one draw needn't show every extreme that they name: `slot_counts`: at most 32 live slots for each sender and tile pair; every tile receives 32 live rows from exactly one sender and fewer than 32 from each other sender.
All inputs are finite; a program needn't handle non-finite values.
Results may differ from the reference program's by a relative error of at most 0.0046.
Values may be sent and summed in bfloat16 or wider, within the bound.
A program may use at most 64 MiB of HBM per device.

```python
import jax
import jax.numpy as jnp
from jax import lax

CH = 256
HID = 512
TH = 32
TW = 128
CAP = 32
NTILES = 128
CELLS = 4096
N_LAT = 4
N_LON = 32


def draw_slot_counts(key, part):
    first_key, second_key, third_key = jax.random.split(key, 3)
    tiles = NTILES
    level = jax.random.randint(first_key, (tiles,), 1, 5)
    lower = level * CAP // 8
    upper = level * CAP // 4
    flat = jnp.arange(tiles * tiles, dtype=jnp.int32)
    sender = flat // tiles
    owner = flat % tiles
    spread = upper[owner] - lower[owner]
    raw = jax.random.randint(second_key, (tiles * tiles,), 0, 1 << 20)
    base = lower[owner] + raw % spread
    chosen = jax.random.permutation(third_key, tiles)
    return jnp.where(chosen[owner] == sender, CAP, base).astype(jnp.int32)


def with_ends(values, key, low, largest):
    longest = values.shape.index(max(values.shape))
    spots = []
    for shift in (0, 1):
        where = [jax.random.randint(jax.random.fold_in(key, axis), (), 0, length) for axis, length in enumerate(values.shape)]
        where[longest] = (where[longest] + shift) % values.shape[longest]
        spots.append(tuple(where))
    return values.at[spots[0]].set(low).at[spots[1]].set(largest)


def shard_levels(own_key, extent, pieces, least, top_value):
    factor_of = 1.0
    for position, blocks in pieces:
        steps = jax.random.uniform(jax.random.fold_in(jax.random.fold_in(own_key, 6), position), (blocks,), jnp.float32, least / len(pieces), top_value / len(pieces))
        factor_of = factor_of * jnp.repeat(jnp.exp(steps), extent[position] // blocks).reshape((-1,) + (1,) * (len(extent) - 1 - position))
    return factor_of


def gaussian(stream_key, dims, deviation, reach, pieces=(), kind=jnp.bfloat16):
    drawn = deviation * jax.random.normal(stream_key, dims, jnp.float32)
    if pieces:
        drawn = drawn * shard_levels(stream_key, dims, pieces, -0.22, 0.18)
    return jnp.clip(drawn, -reach, reach).astype(kind)


def setup_inputs(seed: int = 0) -> dict:
    keys = jax.random.split(jax.random.key(seed), 9)
    observations = gaussian(keys[0], (NTILES * NTILES, CAP, CH), 1.0, 6.0, ((0, 128),))
    slot_cells = with_ends(jax.random.randint(keys[1], (NTILES * NTILES, CAP), 0, CELLS), jax.random.fold_in(keys[1], 1), 0, CELLS - 1).astype(jnp.int32)
    slot_counts = draw_slot_counts(jax.random.fold_in(keys[8], 71), 0)
    conv_in = gaussian(keys[3], (3, 3, CH, HID), (9 * CH) ** -0.5, 0.125)
    conv_density = gaussian(keys[4], (3, 3, HID), 3 ** -0.5, 3.5, (), jnp.float32)
    bias_in = gaussian(keys[5], (HID,), 0.5, 3.0, (), jnp.float32)
    conv_mid = gaussian(keys[6], (3, 3, HID, HID), (9 * HID) ** -0.5, 0.09375)
    bias_mid = gaussian(keys[7], (HID,), 0.5, 3.0, (), jnp.float32)
    return dict(observations=observations, slot_cells=slot_cells, slot_counts=slot_counts, conv_in=conv_in, conv_density=conv_density, bias_in=bias_in, conv_mid=conv_mid, bias_mid=bias_mid)


def strided(padded, weight, rows, cols):
    total = jnp.zeros((rows * cols, weight.shape[-1]), jnp.float32)
    for a in range(3):
        for b in range(3):
            tap = padded[a:a + 2 * rows - 1:2, b:b + 2 * cols - 1:2]
            total = total + jnp.dot(tap.reshape(rows * cols, -1), weight[a, b], preferred_element_type=jnp.float32)
    return total.reshape(rows, cols, -1)


def density_term(padded, weight, rows, cols):
    total = jnp.zeros((rows, cols, weight.shape[-1]), jnp.float32)
    for a in range(3):
        for b in range(3):
            tap = padded[a:a + 2 * rows - 1:2, b:b + 2 * cols - 1:2].astype(jnp.float32)
            total = total + tap[:, :, None] * weight[a, b].astype(jnp.float32)[None, None, :]
    return total


def pad_low(field):
    field = jnp.concatenate([field[:, -1:], field], axis=1)
    zeros = jnp.zeros((1,) + field.shape[1:], field.dtype)
    return jnp.concatenate([zeros, field], axis=0)


def reference(observations, slot_cells, slot_counts, conv_in, conv_density, bias_in, conv_mid, bias_mid):
    tiles = N_LAT * N_LON
    cells = TH * TW
    obs_four = observations.reshape(tiles, tiles, CAP, CH)
    cell_three = slot_cells.reshape(tiles, tiles, CAP)
    count_two = slot_counts.reshape(tiles, tiles)

    def one_tile(owner):
        feats = obs_four[:, owner].reshape(tiles * CAP, CH).astype(jnp.float32)
        where_to = cell_three[:, owner].reshape(tiles * CAP)
        counts = count_two[:, owner]
        live = (jnp.arange(CAP, dtype=jnp.int32)[None, :] < counts[:, None]).astype(jnp.int32).reshape(tiles * CAP)
        target = jnp.where(live > 0, where_to, cells).astype(jnp.int32)
        sums = jax.ops.segment_sum(feats, target, num_segments=cells + 1)[:cells]
        density = jax.ops.segment_sum(live.astype(jnp.float32), target, num_segments=cells + 1)[:cells]
        mean = (sums / jnp.maximum(density, 1.0)[:, None]).astype(jnp.bfloat16)
        fraction = (density / (1.0 + density)).astype(jnp.bfloat16)
        return mean, fraction

    mean, fraction = lax.map(one_tile, jnp.arange(tiles, dtype=jnp.int32))
    mean = mean.reshape(N_LAT, N_LON, TH, TW, CH).transpose(0, 2, 1, 3, 4).reshape(N_LAT * TH, N_LON * TW, CH)
    fraction = fraction.reshape(N_LAT, N_LON, TH, TW).transpose(0, 2, 1, 3).reshape(N_LAT * TH, N_LON * TW)
    rows = N_LAT * TH // 2
    cols = N_LON * TW // 2
    first = strided(pad_low(mean), conv_in, rows, cols) + density_term(pad_low(fraction), conv_density, rows, cols)
    hidden = jax.nn.gelu(first + bias_in[None, None, :]).astype(jnp.bfloat16)
    second = strided(pad_low(hidden), conv_mid, rows // 2, cols // 2)
    return jax.nn.gelu(second + bias_mid[None, None, :]).astype(jnp.bfloat16)
```

```python
import functools

import jax
import jax.numpy as jnp
from jax import lax
from jax.experimental import pallas as pl
from jax.experimental.pallas import tpu as pltpu
from jax.sharding import PartitionSpec as P

MESH = pl.DeviceIdType.MESH
N = 128
SLOTS = 32
CH = 256
HID = 512
WIDE = CH + 128
GROUPS = 8
PER = N // GROUPS
K1 = 9 * CH
K2 = 9 * HID
F32 = jnp.float32
BF16 = jnp.bfloat16


def position():
    lat = lax.axis_index("lat")
    lon = lax.axis_index("lon")
    return lon & 3, ((lat >> 1) << 1) + (lon >> 4), (lon >> 2) & 3, lat & 1


def partner(here, bb, cc, aa, dc, sign):
    x, y, z, core = here
    x = (x + sign * aa) & 3
    y = (y + sign * (aa + bb)) & 3
    z = (z + sign * (aa + cc)) & 3
    core = core ^ dc
    return (y & 2) + core, ((y & 1) << 4) + (z << 2) + x


def gelu(x):
    return 0.5 * x * (1.0 + jnp.tanh(0.7978845608028654 * (x + 0.044715 * (x * x * x))))


def one_hot(ids, tag, want, height):
    if tag is not None:
        ids = jnp.where(tag == want, ids, jnp.full_like(ids, -1.0))
    rows = lax.broadcasted_iota(jnp.int32, (height, 128), 0).astype(F32).astype(BF16)
    rows = rows.reshape(height // 16, 16, 128)
    hit = rows == ids[None]
    return jnp.where(hit, jnp.ones_like(rows), jnp.zeros_like(rows)).reshape(height, 128)


def first_row(block, row):
    sub = lax.broadcasted_iota(jnp.int32, block.shape, 0)
    return jnp.where(sub == 0, jnp.broadcast_to(row, block.shape), block)


def down_one(block, row):
    return first_row(pltpu.roll(block, 1, 0), row)


def offset(q, ip, i):
    return ip * (576 if q else 512) + i * 64


def kernel(
    obs, cells, counts, w1, wd, b1, w2, b2, out,
    rows_in, meta_out, meta_in, acc, dens, edge, edge_bf, corner, corner_bf, top_in, left_in, corner_in,
    x0, x1, xe, hid0, hid1, ext, w1v, w2v, wdf,
    send, recv, msend, mrecv, wsem, hsend, hrecv,
):
    here = position()
    lat = lax.axis_index("lat")
    lon = lax.axis_index("lon")

    def each(fn):
        for i in range(8):
            fn(i, 0, 0, i >> 1, i & 1)

        def body(o, carry):
            for i in range(8):
                fn(o * 8 + i, o >> 2, o & 3, i >> 1, i & 1)
            return carry

        lax.fori_loop(1, 16, body, 0)

    barrier = pltpu.get_barrier_semaphore()

    def greet(k, bb, cc, aa, dc):
        if isinstance(k, int) and k == 0:
            return
        pl.semaphore_signal(
            barrier, inc=1, device_id=partner(here, bb, cc, aa, dc, -1), device_id_type=MESH
        )

    each(greet)
    w1_copy = pltpu.make_async_copy(w1, w1v.at[pl.ds(0, K1)], wsem.at[0])
    w2_copy = pltpu.make_async_copy(w2, w2v, wsem.at[1])
    w1_copy.start()
    w2_copy.start()

    lane = lax.broadcasted_iota(jnp.int32, (N, 128), 1)
    sub = lax.broadcasted_iota(jnp.int32, (N, 128), 0)
    column = jnp.sum(
        jnp.where(lane == sub, jnp.broadcast_to(counts[...], (N, 128)), 0), axis=1, keepdims=True
    )
    cell_block = cells[...]
    wide_cells = jnp.concatenate([cell_block] * 4, axis=1)
    coded = jnp.where((lane & 31) < column, wide_cells, -1)
    for v in range(4):
        meta_out[v] = jnp.where((lane >> 5) == v, coded, 0).reshape(N, 1, 128)
    acc[...] = jnp.zeros_like(acc)
    dens[...] = jnp.zeros_like(dens)
    edge[...] = jnp.zeros_like(edge)
    wdf[...] = jnp.zeros_like(wdf)
    wdf[0:9, :] = wd[...]
    taps = wdf[...]
    taps_hi = taps.astype(BF16)
    taps_lo = (taps - taps_hi.astype(F32)).astype(BF16)
    w1v[pl.ds(K1, 128), :] = jnp.concatenate(
        [taps_hi, taps_lo, jnp.zeros((96, HID), BF16)], axis=0
    )

    pl.semaphore_wait(barrier, N - 1)

    def dispatch(k, bb, cc, aa, dc):
        to_lat, to_lon = partner(here, bb, cc, aa, dc, 1)
        to = to_lat * 32 + to_lon
        v = (aa * 2 + dc) & 3
        if isinstance(k, int) and k == 0:
            pltpu.make_async_copy(meta_out.at[v, pl.ds(to, 1)], meta_in.at[pl.ds(0, 1)], mrecv.at[0]).start()
            pltpu.make_async_copy(obs.at[pl.ds(to, 1)], rows_in.at[pl.ds(0, 1)], recv.at[0]).start()
            return
        pltpu.make_async_remote_copy(
            src_ref=meta_out.at[v, pl.ds(to, 1)], dst_ref=meta_in.at[pl.ds(k, 1)],
            send_sem=msend, recv_sem=mrecv.at[k // PER],
            device_id=(to_lat, to_lon), device_id_type=MESH,
        ).start()
        pltpu.make_async_remote_copy(
            src_ref=obs.at[pl.ds(to, 1)], dst_ref=rows_in.at[pl.ds(k, 1)],
            send_sem=send, recv_sem=recv.at[k // PER],
            device_id=(to_lat, to_lon), device_id_type=MESH,
        ).start()

    each(dispatch)

    def spread(v):
        return jnp.broadcast_to(v.astype(F32), (16, 128)).astype(BF16)

    def codes(g):
        result = []
        for t in range(4):
            cell = sum(meta_in[g * PER + 4 * t + u] for u in range(4))
            alive = cell >= 0
            r = cell >> 7
            c = cell & 127
            col = (c & 1) * 64 + ((c >> 1) & 1) * 32 + (c >> 2)
            row = (r & 1) * 16 + ((r >> 1) & 1) * 8 + (r >> 2)
            pos = (
                (r & 1) * 2048 + (c & 1) * 1024 + ((r >> 1) & 1) * 512 + (r >> 2) * 64
                + ((c >> 1) & 1) * 32 + (c >> 2)
            )
            result.append(
                (
                    spread(pos & 255),
                    spread(jnp.where(alive, pos >> 8, 99)),
                    spread(pos & 127),
                    spread(jnp.where(alive, pos >> 7, 199)),
                    spread(col),
                    spread(jnp.where(alive, r - 29, 99)),
                    spread(jnp.where(alive & (c >= 125), (c - 125) * 32 + row, -1)),
                )
            )
        return result

    def gather_edges(code, block):
        wide = jnp.concatenate([block, jnp.ones((PER * SLOTS, 128), BF16)], axis=1)
        for e in range(4):
            if e < 3:
                hot = [one_hot(code[t][4], code[t][5], e, 128) for t in range(4)]
            else:
                hot = [one_hot(code[t][6], None, None, 128) for t in range(4)]
            at = pl.ds(e * 128, 128)
            edge[at, :] += jnp.dot(jnp.concatenate(hot, axis=1), wide, preferred_element_type=F32)

    def gather_cells(code, block):
        lows = jnp.concatenate([one_hot(code[t][2], None, None, 128) for t in range(4)], axis=1)
        highs = jnp.concatenate([one_hot(code[t][3], None, None, 128) for t in range(4)], axis=1)
        dens[...] += lax.dot_general(lows, highs, (((1,), (1,)), ((), ())), preferred_element_type=F32)
        for b in range(16):
            hot = jnp.concatenate([one_hot(code[t][0], code[t][1], b, 256) for t in range(4)], axis=1)
            at = pl.ds(b * 256, 256)
            acc[at, :] += jnp.dot(hot, block, preferred_element_type=F32)

    def arrived(g):
        pltpu.make_async_copy(
            meta_out.at[0, pl.ds(g * PER, PER)], meta_in.at[pl.ds(g * PER, PER)], mrecv.at[g]
        ).wait()
        pltpu.make_async_copy(
            obs.at[pl.ds(g * PER, PER)], rows_in.at[pl.ds(g * PER, PER)], recv.at[g]
        ).wait()
        return codes(g), rows_in[pl.ds(g * PER, PER)].reshape(PER * SLOTS, CH)

    def group(g, carry):
        code, block = arrived(g)
        gather_edges(code, block)
        gather_cells(code, block)
        return carry

    lax.fori_loop(0, GROUPS - 1, group, 0)
    code, block = arrived(GROUPS - 1)
    gather_edges(code, block)

    amount = edge[:, CH:]
    scale = 1.0 / jnp.maximum(amount, 1.0)
    edge[...] = jnp.concatenate(
        [edge[:, 0:128] * scale, edge[:, 128:CH] * scale, amount / (1.0 + amount)], axis=1
    )
    edge_bf[...] = edge[...].astype(BF16)
    corner[...] = jnp.zeros_like(corner)
    for a in range(3):
        for b, at in enumerate((95, 63, 127)):
            corner[pl.ds(a * 3 + b, 1), :] = edge[pl.ds(a * 128 + at, 1), :]
    corner_bf[...] = corner[...].astype(BF16)
    next_lat = (lat + 1) & 3
    next_lon = (lon + 1) & 31
    halos = [
        pltpu.make_async_remote_copy(
            src_ref=src, dst_ref=dst, send_sem=hsend.at[i], recv_sem=hrecv.at[i],
            device_id=to, device_id_type=MESH,
        )
        for i, (src, dst, to) in enumerate(
            (
                (edge_bf.at[pl.ds(0, 384)], top_in, (next_lat, lon)),
                (edge_bf.at[pl.ds(384, 96)], left_in, (lat, next_lon)),
                (corner_bf, corner_in, (next_lat, next_lon)),
            )
        )
    ]
    for halo in halos:
        halo.start()

    gather_cells(code, block)

    count = dens[...]
    scale_all = 1.0 / jnp.maximum(count, 1.0)
    fraction_all = count / (1.0 + count)
    for h in range(32):
        scale = jnp.broadcast_to(scale_all[:, h : h + 1], (128, 128))
        fraction = jnp.broadcast_to(fraction_all[:, h : h + 1], (128, 128))
        sums = acc[pl.ds(h * 128, 128), :]
        value = jnp.concatenate([sums[:, 0:128] * scale, sums[:, 128:CH] * scale, fraction], axis=1)
        q, p, ip, i = h >> 4, (h >> 3) & 1, (h >> 2) & 1, (h & 3) * 2
        x = x1 if q else x0
        x[p, pl.ds(offset(q, ip, i), 128), :] = value.astype(BF16)
        if p:
            for half in range(2):
                part = value[half * 64 : half * 64 + 64]
                moved = jnp.concatenate([pltpu.roll(part[32:64], 1, 0), part[0:32]], axis=0)
                x[2, pl.ds(offset(q, ip, i + half), 64), :] = moved.astype(BF16)

    for halo in halos:
        halo.wait()

    inside = jnp.where(lat > 0, 1.0, 0.0).astype(F32)
    left = left_in[...].astype(F32)
    diag = corner_in[...].astype(F32) * inside
    for a in range(3):
        p0 = top_in[pl.ds(a * 128, 64), :].astype(F32) * inside
        p1 = top_in[pl.ds(a * 128 + 64, 64), :].astype(F32) * inside
        moved = jnp.concatenate([down_one(p1[32:64], diag[a * 3 + 2 : a * 3 + 3]), p1[0:32]], axis=0)
        for b, top in enumerate((moved, p0, p1)):
            side = left[b * 32 : b * 32 + 32]
            if a == 0:
                side = jnp.concatenate([down_one(side[24:32], diag[6 + b : 7 + b]), side[16:24]], axis=0)
            else:
                side = side[(a - 1) * 16 : a * 16]
            angle = first_row(jnp.zeros((16, WIDE), F32), diag[a * 3 + b : a * 3 + b + 1])
            top = top.astype(BF16)
            xe[a * 3 + b, pl.ds(0, 64), :] = top
            xe[a * 3 + b, pl.ds(64, 16), :] = side.astype(BF16)
            xe[a * 3 + b, pl.ds(80, 16), :] = angle.astype(BF16)
            if a == 2:
                x1[(2, 0, 1)[b], pl.ds(512, 64), :] = top
    for q in range(2):
        x = x1 if q else x0
        for ip in range(2):
            for i in range(8):
                at = pl.ds(offset(q, ip, i), 16)
                t = 64 + q * 16 + ip * 8 + i
                x[2, at, :] = first_row(x[2, at, :].astype(F32), left[t : t + 1]).astype(BF16)

    w1_copy.wait()
    lanes = lax.broadcasted_iota(jnp.int32, (16, 128), 1)
    tap_of_lane = jnp.where(lanes < 32, lanes & 15, 99).astype(F32).astype(BF16)
    bias1 = b1[...]
    for chunk in range(4):
        ip, half = chunk >> 1, chunk & 1
        parts = []
        shares = None
        for a in range(3):
            for b in range(3):
                v = (2, 0, 1)[b]
                if a == 1:
                    x, at = x0, ip * 512 + half * 256
                elif a == 2:
                    x, at = x1, ip * 576 + half * 256
                else:
                    x, at = x1, (0 if ip else 512) + half * 256
                data = x[v, pl.ds(at, 256), :]
                if chunk == 0:
                    data = jnp.concatenate([xe[a * 3 + b], data], axis=0)
                parts.append(data[:, 0:CH])
                share = data[:, CH:].reshape(-1, 16, 128)
                if shares is None:
                    shares = jnp.zeros_like(share)
                shares = jnp.where((tap_of_lane == a * 3 + b)[None], share, shares)
        parts.append(shares.reshape(-1, 128))
        first = jnp.dot(jnp.concatenate(parts, axis=1), w1v[...], preferred_element_type=F32)
        hidden = gelu(first + bias1)
        if chunk == 0:
            ext[...] = hidden[0:96]
            hidden = hidden[96:]
            above0 = ext[pl.ds(0, 32), :] * inside
            above1 = ext[pl.ds(32, 32), :] * inside
            hid1[0, pl.ds(0, 32), :] = above0.astype(BF16)
            hid1[1, pl.ds(0, 32), :] = above1.astype(BF16)
            hid1[2, pl.ds(0, 32), :] = down_one(above1, ext[pl.ds(80, 1), :] * inside).astype(BF16)
        hid = hid1 if ip else hid0
        for k in range(4):
            i = half * 4 + k
            at = pl.ds(i * 32 + (32 if ip else 0), 32)
            even = hidden[k * 64 : k * 64 + 32]
            odd = hidden[k * 64 + 32 : k * 64 + 64]
            hid[0, at, :] = even.astype(BF16)
            hid[1, at, :] = odd.astype(BF16)
            hid[2, at, :] = down_one(odd, ext[pl.ds(64 + ip * 8 + i, 1), :]).astype(BF16)

    w2_copy.wait()
    parts = []
    for a in range(3):
        for b in range(3):
            v = (2, 0, 1)[b]
            if a == 1:
                parts.append(hid0[v])
            else:
                parts.append(hid1[v, pl.ds(32 if a == 2 else 0, 256), :])
    second = jnp.dot(jnp.concatenate(parts, axis=1), w2v[...], preferred_element_type=F32)
    out[...] = gelu(second + b2[...]).astype(BF16).reshape(8, 32, HID)

    pltpu.make_async_copy(obs.at[pl.ds(1, N - 1)], rows_in.at[pl.ds(1, N - 1)], send).wait()
    pltpu.make_async_copy(
        meta_out.at[0, pl.ds(1, N - 1)], meta_in.at[pl.ds(1, N - 1)], msend
    ).wait()


def on_device(obs, cells, counts, conv_in, conv_density, bias_in, conv_mid, bias_mid):
    vmem = pl.BlockSpec(memory_space=pltpu.VMEM)
    hbm = pl.BlockSpec(memory_space=pl.ANY)
    dma = pltpu.SemaphoreType.DMA
    return pl.pallas_call(
        kernel,
        out_shape=jax.ShapeDtypeStruct((8, 32, HID), BF16),
        in_specs=[hbm, vmem, vmem, hbm, vmem, vmem, hbm, vmem],
        out_specs=vmem,
        scratch_shapes=[
            pltpu.VMEM((N, SLOTS, CH), BF16),
            pltpu.VMEM((4, N, 1, 128), jnp.int32),
            pltpu.VMEM((N, 1, 128), jnp.int32),
            pltpu.VMEM((4096, CH), F32),
            pltpu.VMEM((128, 128), F32),
            pltpu.VMEM((512, WIDE), F32),
            pltpu.VMEM((512, WIDE), BF16),
            pltpu.VMEM((16, WIDE), F32),
            pltpu.VMEM((16, WIDE), BF16),
            pltpu.VMEM((384, WIDE), BF16),
            pltpu.VMEM((96, WIDE), BF16),
            pltpu.VMEM((16, WIDE), BF16),
            pltpu.VMEM((3, 1024, WIDE), BF16),
            pltpu.VMEM((3, 1088, WIDE), BF16),
            pltpu.VMEM((9, 96, WIDE), BF16),
            pltpu.VMEM((3, 256, HID), BF16),
            pltpu.VMEM((3, 288, HID), BF16),
            pltpu.VMEM((96, HID), F32),
            pltpu.VMEM((K1 + 128, HID), BF16),
            pltpu.VMEM((K2, HID), BF16),
            pltpu.VMEM((16, HID), F32),
            dma,
            dma((GROUPS,)),
            dma,
            dma((GROUPS,)),
            dma((2,)),
            dma((3,)),
            dma((3,)),
        ],
        compiler_params=pltpu.CompilerParams(
            collective_id=0, has_side_effects=True, vmem_limit_bytes=56 * 2**20
        ),
    )(
        obs,
        cells,
        counts.reshape(1, N),
        conv_in.reshape(K1, HID),
        conv_density.reshape(9, HID),
        bias_in.reshape(1, HID),
        conv_mid.reshape(K2, HID),
        bias_mid.reshape(1, HID),
    )


def solution(mesh):
    return jax.shard_map(
        on_device,
        mesh=mesh,
        in_specs=(
            P(("lat", "lon"), None, None),
            P(("lat", "lon"), None),
            P(("lat", "lon")),
            P(),
            P(),
            P(),
            P(),
            P(),
        ),
        out_specs=P("lat", "lon", None),
        check_vma=False,
    )
```

```python
import functools

import jax
import jax.numpy as jnp
from jax import lax
from jax.experimental import pallas as pl
from jax.experimental.pallas import tpu as pltpu
from jax.sharding import PartitionSpec as P

MESH = pl.DeviceIdType.MESH
N = 128
SLOTS = 32
CH = 256
HID = 512
WIDE = CH + 128
PER = 8
GROUPS = N // PER
K1 = 9 * CH
K2 = 9 * HID
F32 = jnp.float32
BF16 = jnp.bfloat16


def position():
    lat = lax.axis_index("lat")
    lon = lax.axis_index("lon")
    return lon & 3, ((lat >> 1) << 1) + (lon >> 4), (lon >> 2) & 3, lat & 1


def partner(here, bb, cc, aa, dc, sign):
    x, y, z, core = here
    x = (x + sign * aa) & 3
    y = (y + sign * (aa + bb)) & 3
    z = (z + sign * (aa + cc)) & 3
    core = core ^ dc
    return (y & 2) + core, ((y & 1) << 4) + (z << 2) + x


def gelu(x):
    return 0.5 * x * (1.0 + jnp.tanh(0.7978845608028654 * (x + 0.044715 * (x * x * x))))


def one_hot(ids, tag, want, height):
    if tag is not None:
        ids = jnp.where(tag == want, ids, jnp.full_like(ids, -1.0))
    rows = lax.broadcasted_iota(jnp.int32, (height, 128), 0).astype(F32).astype(BF16)
    rows = rows.reshape(height // 16, 16, 128)
    hit = rows == ids[None]
    return jnp.where(hit, jnp.ones_like(rows), jnp.zeros_like(rows)).reshape(height, 128)


def first_row(block, row):
    sub = lax.broadcasted_iota(jnp.int32, block.shape, 0)
    return jnp.where(sub == 0, jnp.broadcast_to(row, block.shape), block)


def down_one(block, row):
    return first_row(pltpu.roll(block, 1, 0), row)


def offset(q, ip, i):
    return ip * (576 if q else 512) + i * 64


def kernel(
    obs, cells, counts, w1, wd, b1, w2, b2, out,
    rows_in, meta_out, meta_in, acc, dens, edge, edge_bf, edge_dens, edge_fr, edge_fr_bf, corner, corner_bf,
    top_in, left_in, corner_in, top_fr, left_fr,
    x0, x1, xe, hid0, hid1, ext, pre_top, pre_left, w1v, w2v, wdf,
    send, recv, msend, mrecv, wsem, hsend, hrecv,
):
    here = position()
    lat = lax.axis_index("lat")
    lon = lax.axis_index("lon")

    def each(fn):
        for i in range(8):
            fn(i, 0, 0, i >> 1, i & 1)

        def body(o, carry):
            for i in range(8):
                fn(o * 8 + i, o >> 2, o & 3, i >> 1, i & 1)
            return carry

        lax.fori_loop(1, 16, body, 0)

    barrier = pltpu.get_barrier_semaphore()

    def greet(k, bb, cc, aa, dc):
        if isinstance(k, int) and k == 0:
            return
        pl.semaphore_signal(
            barrier, inc=1, device_id=partner(here, bb, cc, aa, dc, -1), device_id_type=MESH
        )

    each(greet)
    w1_copy = pltpu.make_async_copy(w1, w1v.at[pl.ds(0, K1)], wsem.at[0])
    w2_copy = pltpu.make_async_copy(w2, w2v, wsem.at[1])
    w1_copy.start()
    w2_copy.start()

    lane = lax.broadcasted_iota(jnp.int32, (N, 128), 1)
    slot = lax.broadcasted_iota(jnp.int32, (SLOTS, N), 0)
    coded = jnp.where(slot < counts[...], cells[...], -1)
    coded = jnp.transpose(jnp.concatenate([coded] * 4, axis=0))
    for v in range(4):
        meta_out[v] = jnp.where((lane >> 5) == v, coded, 0).reshape(N, 1, 128)
    acc[...] = jnp.zeros_like(acc)
    dens[...] = jnp.zeros_like(dens)
    edge[...] = jnp.zeros_like(edge)
    edge_dens[...] = jnp.zeros_like(edge_dens)
    x1[:, pl.ds(512, 64), :] = jnp.zeros((3, 64, WIDE), BF16)
    wdf[...] = jnp.zeros_like(wdf)
    for a in range(3):
        wdf[3 * a : 3 * a + 3, :] = wd[a]
    taps = wdf[...]
    taps_hi = taps.astype(BF16)
    taps_lo = (taps - taps_hi.astype(F32)).astype(BF16)
    w1v[pl.ds(K1, 128), :] = jnp.concatenate(
        [taps_hi, taps_lo, jnp.zeros((96, HID), BF16)], axis=0
    )

    pl.semaphore_wait(barrier, N - 1)

    def dispatch(k, bb, cc, aa, dc):
        to_lat, to_lon = partner(here, bb, cc, aa, dc, 1)
        to = to_lat * 32 + to_lon
        v = (aa * 2 + dc) & 3
        if isinstance(k, int) and k == 0:
            pltpu.make_async_copy(meta_out.at[v, pl.ds(to, 1)], meta_in.at[pl.ds(0, 1)], mrecv.at[0]).start()
            pltpu.make_async_copy(obs.at[pl.ds(to, 1)], rows_in.at[pl.ds(0, 1)], recv.at[0]).start()
            return
        pltpu.make_async_remote_copy(
            src_ref=meta_out.at[v, pl.ds(to, 1)], dst_ref=meta_in.at[pl.ds(k, 1)],
            send_sem=msend, recv_sem=mrecv.at[k // PER],
            device_id=(to_lat, to_lon), device_id_type=MESH,
        ).start()
        pltpu.make_async_remote_copy(
            src_ref=obs.at[pl.ds(to, 1)], dst_ref=rows_in.at[pl.ds(k, 1)],
            send_sem=send, recv_sem=recv.at[k // PER],
            device_id=(to_lat, to_lon), device_id_type=MESH,
        ).start()

    each(dispatch)

    def spread(v):
        return jnp.broadcast_to(v.astype(F32), (16, 128)).astype(BF16)

    def codes(start, count):
        result = []
        for t in range(count // 4):
            cell = sum(meta_in[start + 4 * t + u] for u in range(4))
            alive = cell >= 0
            r = cell >> 7
            c = cell & 127
            col = (c & 1) * 64 + ((c >> 1) & 1) * 32 + (c >> 2)
            row = (r & 1) * 16 + ((r >> 1) & 1) * 8 + (r >> 2)
            pos = (
                (r & 1) * 2048 + (c & 1) * 1024 + ((r >> 1) & 1) * 512 + (r >> 2) * 64
                + ((c >> 1) & 1) * 32 + (c >> 2)
            )
            result.append(
                (
                    spread(pos & 255),
                    spread(jnp.where(alive, pos >> 8, 99)),
                    spread(pos & 127),
                    spread(jnp.where(alive, pos >> 7, 199)),
                    spread(col),
                    spread(jnp.where(alive, r - 29, 99)),
                    spread(jnp.where(alive & (c >= 125), (c - 125) * 32 + row, -1)),
                )
            )
        return result

    def across(code, which, tag, want, height):
        return jnp.concatenate(
            [one_hot(c[which], None if tag is None else c[tag], want, height) for c in code], axis=1
        )

    def dot_t(left, right):
        return lax.dot_general(left, right, (((1,), (1,)), ((), ())), preferred_element_type=F32)

    def gather_edges(code, block):
        rows = across(code, 5, None, None, 16)
        edge_dens[0:16, :] += dot_t(rows, across(code, 4, None, None, 128))
        last = across(code, 6, None, None, 128)
        edge_dens[16:32, :] += dot_t(jnp.ones_like(rows), last)
        for e in range(4):
            hot = across(code, 4, 5, e, 128) if e < 3 else last
            at = pl.ds(e * 128, 128)
            edge[at, :] += jnp.dot(hot, block, preferred_element_type=F32)

    def gather_cells(code, block):
        dens[...] += dot_t(across(code, 2, None, None, 128), across(code, 3, None, None, 128))
        for b in range(16):
            at = pl.ds(b * 256, 256)
            acc[at, :] += jnp.dot(across(code, 0, 1, b, 256), block, preferred_element_type=F32)

    def arrived(g, size):
        start = g * PER
        for u in range(size):
            one = pl.ds(start + u * PER, PER)
            pltpu.make_async_copy(meta_out.at[0, one], meta_in.at[one], mrecv.at[g + u]).wait()
            pltpu.make_async_copy(obs.at[one], rows_in.at[one], recv.at[g + u]).wait()
        count = size * PER
        return codes(start, count), rows_in[pl.ds(start, count)].reshape(count * SLOTS, CH)

    def group(g, carry):
        code, block = arrived(g * 2, 2)
        gather_edges(code, block)
        gather_cells(code, block)
        return carry

    lax.fori_loop(0, GROUPS // 2 - 1, group, 0)
    code, block = arrived(GROUPS - 2, 1)
    gather_edges(code, block)
    gather_cells(code, block)
    code, block = arrived(GROUPS - 1, 1)
    gather_edges(code, block)

    sub16 = lax.broadcasted_iota(jnp.int32, (16, 128), 0)
    amount = jnp.where(sub16 == 3, edge_dens[16:32, :], edge_dens[0:16, :])
    edge_fr_bf[...] = (amount / (1.0 + amount)).astype(BF16)
    amount = jnp.transpose(jnp.concatenate([amount, jnp.zeros((112, 128), F32)], axis=0))
    scales = 1.0 / jnp.maximum(amount, 1.0)
    fractions = amount / (1.0 + amount)
    for e in range(4):
        scale = jnp.broadcast_to(scales[:, e : e + 1], (128, 128))
        at = pl.ds(e * 128, 128)
        sums = edge[at, :]
        value = jnp.concatenate([sums[:, 0:128] * scale, sums[:, 128:CH] * scale], axis=1)
        edge[at, :] = value
        edge_bf[at, :] = value.astype(BF16)
        if e < 3:
            edge_fr[at, :] = jnp.broadcast_to(fractions[:, e : e + 1], (128, 128))
    corner[...] = jnp.zeros_like(corner)
    for a in range(3):
        for b, at in enumerate((95, 63, 127)):
            corner[pl.ds(a * 3 + b, 1), 0:CH] = edge[pl.ds(a * 128 + at, 1), :]
            corner[pl.ds(a * 3 + b, 1), CH:WIDE] = edge_fr[pl.ds(a * 128 + at, 1), :]
    corner_bf[...] = corner[...].astype(BF16)
    next_lat = (lat + 1) & 3
    next_lon = (lon + 1) & 31
    halos = [
        pltpu.make_async_remote_copy(
            src_ref=src, dst_ref=dst, send_sem=hsend.at[i], recv_sem=hrecv.at[i],
            device_id=to, device_id_type=MESH,
        )
        for i, (src, dst, to) in enumerate(
            (
                (edge_bf.at[pl.ds(0, 384)], top_in, (next_lat, lon)),
                (edge_bf.at[pl.ds(384, 96)], left_in, (lat, next_lon)),
                (corner_bf, corner_in, (next_lat, next_lon)),
                (edge_fr_bf, top_fr, (next_lat, lon)),
                (edge_fr_bf, left_fr, (lat, next_lon)),
            )
        )
    ]
    for halo in halos:
        halo.start()

    gather_cells(code, block)

    count = dens[...]
    scale_all = 1.0 / jnp.maximum(count, 1.0)
    fraction_all = count / (1.0 + count)
    for h in range(32):
        scale = jnp.broadcast_to(scale_all[:, h : h + 1], (128, 128))
        fraction = jnp.broadcast_to(fraction_all[:, h : h + 1], (128, 128))
        sums = acc[pl.ds(h * 128, 128), :]
        value = jnp.concatenate([sums[:, 0:128] * scale, sums[:, 128:CH] * scale, fraction], axis=1)
        q, p, ip, i = h >> 4, (h >> 3) & 1, (h >> 2) & 1, (h & 3) * 2
        x = x1 if q else x0
        x[p, pl.ds(offset(q, ip, i), 128), :] = value.astype(BF16)
        if p:
            for half in range(2):
                part = value[half * 64 : half * 64 + 64]
                moved = jnp.concatenate([down_one(part[32:64], jnp.zeros((1, WIDE), F32)), part[0:32]], axis=0)
                x[2, pl.ds(offset(q, ip, i + half), 64), :] = moved.astype(BF16)

    w1_copy.wait()
    lanes = lax.broadcasted_iota(jnp.int32, (16, 128), 1)
    tap_of_lane = jnp.where(lanes < 32, lanes & 15, 99).astype(F32).astype(BF16)
    bias1 = b1[...]

    def layer_one(blocks):
        shares = jnp.zeros((blocks[0].shape[0] // 16, 16, 128), BF16)
        for t, data in enumerate(blocks):
            shares = jnp.where((tap_of_lane == t)[None], data[:, CH:].reshape(-1, 16, 128), shares)
        parts = [data[:, 0:CH] for data in blocks] + [shares.reshape(-1, 128)]
        return jnp.dot(jnp.concatenate(parts, axis=1), w1v[...], preferred_element_type=F32)

    for chunk in range(4):
        ip, half = chunk >> 1, chunk & 1
        blocks = []
        for a in range(3):
            for b in range(3):
                v = (2, 0, 1)[b]
                if a == 1:
                    x, at = x0, ip * 512 + half * 256
                elif a == 2:
                    x, at = x1, ip * 576 + half * 256
                else:
                    x, at = x1, (0 if ip else 512) + half * 256
                blocks.append(x[v, pl.ds(at, 256), :])
        first = layer_one(blocks) + bias1
        if chunk == 0:
            pre_top[...] = first[0:64]
        hidden = gelu(first)
        hid = hid1 if ip else hid0
        for k in range(4):
            i = half * 4 + k
            pre_left[pl.ds(ip * 8 + i, 1), :] = first[k * 64 : k * 64 + 1]
            at = pl.ds(i * 32 + (32 if ip else 0), 32)
            odd = hidden[k * 64 + 32 : k * 64 + 64]
            hid[0, at, :] = hidden[k * 64 : k * 64 + 32].astype(BF16)
            hid[1, at, :] = odd.astype(BF16)
            hid[2, at, :] = pltpu.roll(odd, 1, 0).astype(BF16)

    for halo in halos:
        halo.wait()

    inside = jnp.where(lat > 0, 1.0, 0.0).astype(F32)

    def columns(fr):
        return jnp.transpose(jnp.concatenate([fr[...].astype(F32), jnp.zeros((112, 128), F32)], axis=0))

    top_cols = columns(top_fr)
    left_cols = columns(left_fr)
    left = jnp.concatenate(
        [left_in[...].astype(F32), jnp.broadcast_to(left_cols[0:96, 3:4], (96, 128))], axis=1
    )
    diag = corner_in[...].astype(F32) * inside
    for a in range(3):
        rows = jnp.concatenate(
            [
                top_in[pl.ds(a * 128, 128), :].astype(F32),
                jnp.broadcast_to(top_cols[:, a : a + 1], (128, 128)),
            ],
            axis=1,
        ) * inside
        p0, p1 = rows[0:64], rows[64:128]
        moved = jnp.concatenate([down_one(p1[32:64], diag[a * 3 + 2 : a * 3 + 3]), p1[0:32]], axis=0)
        for b, top in enumerate((moved, p0, p1)):
            side = left[b * 32 : b * 32 + 32]
            if a == 0:
                side = jnp.concatenate([down_one(side[24:32], diag[6 + b : 7 + b]), side[16:24]], axis=0)
            else:
                side = side[(a - 1) * 16 : a * 16]
            angle = first_row(jnp.zeros((16, WIDE), F32), diag[a * 3 + b : a * 3 + b + 1])
            xe[a * 3 + b, pl.ds(0, 64), :] = top.astype(BF16)
            xe[a * 3 + b, pl.ds(64, 16), :] = side.astype(BF16)
            xe[a * 3 + b, pl.ds(80, 16), :] = angle.astype(BF16)
    blocks = []
    for a in range(3):
        for b in range(3):
            if a == 0:
                over = xe[6 + b, pl.ds(0, 64), :]
            else:
                over = jnp.zeros((64, WIDE), BF16)
            if b == 0:
                side = xe[a * 3 + 2, pl.ds(64, 16), :]
                if a == 0:
                    side = first_row(side.astype(F32), jnp.zeros((1, WIDE), F32)).astype(BF16)
            else:
                side = jnp.zeros((16, WIDE), BF16)
            blocks.append(jnp.concatenate([xe[a * 3 + b], over, side], axis=0))
    rest = layer_one(blocks)
    ext[...] = gelu(rest[0:96] + bias1)
    above0 = ext[pl.ds(0, 32), :] * inside
    above1 = ext[pl.ds(32, 32), :] * inside
    hid1[0, pl.ds(0, 32), :] = above0.astype(BF16)
    hid1[1, pl.ds(0, 32), :] = above1.astype(BF16)
    hid1[2, pl.ds(0, 32), :] = down_one(above1, ext[pl.ds(80, 1), :] * inside).astype(BF16)
    side = rest[160:176]
    over = rest[96:160] + first_row(jnp.zeros((64, HID), F32), side[0:1])
    over = gelu(pre_top[...] + over)
    side = gelu(pre_left[...] + side)
    hid0[0, pl.ds(0, 32), :] = over[0:32].astype(BF16)
    hid0[1, pl.ds(0, 32), :] = over[32:64].astype(BF16)
    hid0[2, pl.ds(0, 32), :] = down_one(over[32:64], ext[pl.ds(64, 1), :]).astype(BF16)
    for ip in range(2):
        hid = hid1 if ip else hid0
        for i in range(8):
            n = ip * 8 + i
            if n == 0:
                continue
            at = pl.ds(i * 32 + (32 if ip else 0), 16)
            hid[0, at, :] = first_row(hid[0, at, :].astype(F32), side[n : n + 1]).astype(BF16)
            hid[2, at, :] = first_row(hid[2, at, :].astype(F32), ext[pl.ds(64 + n, 1), :]).astype(BF16)

    w2_copy.wait()
    parts = []
    for a in range(3):
        for b in range(3):
            v = (2, 0, 1)[b]
            if a == 1:
                parts.append(hid0[v])
            else:
                parts.append(hid1[v, pl.ds(32 if a == 2 else 0, 256), :])
    second = jnp.dot(jnp.concatenate(parts, axis=1), w2v[...], preferred_element_type=F32)
    out[...] = gelu(second + b2[...]).astype(BF16).reshape(8, 32, HID)

    pltpu.make_async_copy(obs.at[pl.ds(1, N - 1)], rows_in.at[pl.ds(1, N - 1)], send).wait()
    pltpu.make_async_copy(
        meta_out.at[0, pl.ds(1, N - 1)], meta_in.at[pl.ds(1, N - 1)], msend
    ).wait()


def on_device(obs, cells, counts, conv_in, conv_density, bias_in, conv_mid, bias_mid):
    vmem = pl.BlockSpec(memory_space=pltpu.VMEM)
    hbm = pl.BlockSpec(memory_space=pl.ANY)
    dma = pltpu.SemaphoreType.DMA
    return pl.pallas_call(
        kernel,
        out_shape=jax.ShapeDtypeStruct((8, 32, HID), BF16),
        in_specs=[hbm, vmem, vmem, hbm, vmem, vmem, hbm, vmem],
        out_specs=vmem,
        scratch_shapes=[
            pltpu.VMEM((N, SLOTS, CH), BF16),
            pltpu.VMEM((4, N, 1, 128), jnp.int32),
            pltpu.VMEM((N, 1, 128), jnp.int32),
            pltpu.VMEM((4096, CH), F32),
            pltpu.VMEM((128, 128), F32),
            pltpu.VMEM((512, CH), F32),
            pltpu.VMEM((512, CH), BF16),
            pltpu.VMEM((32, 128), F32),
            pltpu.VMEM((384, 128), F32),
            pltpu.VMEM((16, 128), BF16),
            pltpu.VMEM((16, WIDE), F32),
            pltpu.VMEM((16, WIDE), BF16),
            pltpu.VMEM((384, CH), BF16),
            pltpu.VMEM((96, CH), BF16),
            pltpu.VMEM((16, WIDE), BF16),
            pltpu.VMEM((16, 128), BF16),
            pltpu.VMEM((16, 128), BF16),
            pltpu.VMEM((3, 1024, WIDE), BF16),
            pltpu.VMEM((3, 1088, WIDE), BF16),
            pltpu.VMEM((9, 96, WIDE), BF16),
            pltpu.VMEM((3, 256, HID), BF16),
            pltpu.VMEM((3, 288, HID), BF16),
            pltpu.VMEM((96, HID), F32),
            pltpu.VMEM((64, HID), F32),
            pltpu.VMEM((16, HID), F32),
            pltpu.VMEM((K1 + 128, HID), BF16),
            pltpu.VMEM((K2, HID), BF16),
            pltpu.VMEM((16, HID), F32),
            dma,
            dma((GROUPS,)),
            dma,
            dma((GROUPS,)),
            dma((2,)),
            dma((5,)),
            dma((5,)),
        ],
        compiler_params=pltpu.CompilerParams(
            collective_id=0, has_side_effects=True, vmem_limit_bytes=56 * 2**20
        ),
    )(
        obs,
        cells.T,
        counts.reshape(1, N),
        conv_in.reshape(K1, HID),
        conv_density,
        bias_in.reshape(1, HID),
        conv_mid.reshape(K2, HID),
        bias_mid.reshape(1, HID),
    )


def solution(mesh):
    return jax.shard_map(
        on_device,
        mesh=mesh,
        in_specs=(
            P(("lat", "lon"), None, None),
            P(("lat", "lon"), None),
            P(("lat", "lon")),
            P(),
            P(),
            P(),
            P(),
            P(),
        ),
        out_specs=P("lat", "lon", None),
        check_vma=False,
    )
```

```python
import functools

import jax
import jax.numpy as jnp
from jax import lax
from jax.experimental import pallas as pl
from jax.experimental.pallas import tpu as pltpu
from jax.sharding import PartitionSpec as P

MESH = pl.DeviceIdType.MESH
N = 128
SLOTS = 32
CH = 256
HID = 512
WIDE = CH + 128
PER = 8
GROUPS = N // PER
K1 = 9 * CH
K2 = 9 * HID
F32 = jnp.float32
BF16 = jnp.bfloat16


def position():
    lat = lax.axis_index("lat")
    lon = lax.axis_index("lon")
    return lon & 3, ((lat >> 1) << 1) + (lon >> 4), (lon >> 2) & 3, lat & 1


def around(v, d):
    return (v + d) & 3


def wrapped(v):
    return jnp.where(v > 2, v - 2, v + 1) if not isinstance(v, int) else v % 3 + 1


def gelu(x):
    return 0.5 * x * (1.0 + jnp.tanh(0.7978845608028654 * (x + 0.044715 * (x * x * x))))


def one_hot(ids, tag, want, height):
    if tag is not None:
        ids = jnp.where(tag == want, ids, jnp.full_like(ids, -1.0))
    rows = lax.broadcasted_iota(jnp.int32, (height, 128), 0).astype(F32).astype(BF16)
    rows = rows.reshape(height // 16, 16, 128)
    hit = rows == ids[None]
    return jnp.where(hit, jnp.ones_like(rows), jnp.zeros_like(rows)).reshape(height, 128)


def first_row(block, row):
    sub = lax.broadcasted_iota(jnp.int32, block.shape, 0)
    return jnp.where(sub == 0, jnp.broadcast_to(row, block.shape), block)


def down_one(block, row):
    return first_row(pltpu.roll(block, 1, 0), row)


def offset(q, ip, i):
    return ip * (576 if q else 512) + i * 64


def kernel(
    obs, cells, counts, w1, wd, b1, w2, b2, out,
    rows_in, meta_out, meta_in, acc, dens, edge, edge_bf, edge_dens, edge_fr, edge_fr_bf, corner, corner_bf,
    top_in, left_in, corner_in, top_fr, left_fr,
    x0, x1, xe, hid0, hid1, ext, pre_top, pre_left, w1v, w2v, wdf,
    entered, send, recv, msend, mrecv, wsem, hsend, hrecv,
):
    x_me, y_me, z_me, core_me = position()
    lat = lax.axis_index("lat")
    lon = lax.axis_index("lon")

    def device(dx, dy, dz, dc):
        y = around(y_me, dy)
        core = core_me ^ dc
        return (y & 2) + core, ((y & 1) << 4) + (around(z_me, dz) << 2) + around(x_me, dx)

    def signal(sem, offsets):
        for to in offsets:
            pl.semaphore_signal(sem, inc=1, device_id=device(*to), device_id_type=MESH)

    barrier = pltpu.get_barrier_semaphore()
    steps = (1, 2, 3)
    x_line = [(d, 0, 0, 0) for d in steps]
    y_line = [(0, d, 0, 0) for d in steps]
    z_line = [(0, 0, d, 0) for d in steps]
    lines = [(0, 0, 0, 1)] + [o[:3] + (c,) for o in x_line + y_line + z_line for c in (0, 1)]
    signal(barrier, lines)
    w1_copy = pltpu.make_async_copy(w1, w1v.at[pl.ds(0, K1)], wsem.at[0])
    w2_copy = pltpu.make_async_copy(w2, w2v, wsem.at[1])
    w1_copy.start()
    w2_copy.start()

    lane = lax.broadcasted_iota(jnp.int32, (N, 128), 1)
    slot = lax.broadcasted_iota(jnp.int32, (SLOTS, N), 0)
    coded = jnp.where(slot < counts[...], cells[...], -1)
    coded = jnp.transpose(jnp.concatenate([coded] * 4, axis=0))
    for v in range(4):
        meta_out[v] = jnp.where((lane >> 5) == v, coded, 0).reshape(N, 1, 128)
    acc[...] = jnp.zeros_like(acc)
    dens[...] = jnp.zeros_like(dens)
    edge[...] = jnp.zeros_like(edge)
    edge_dens[...] = jnp.zeros_like(edge_dens)
    x1[:, pl.ds(512, 64), :] = jnp.zeros((3, 64, WIDE), BF16)
    wdf[...] = jnp.zeros_like(wdf)
    for a in range(3):
        wdf[3 * a : 3 * a + 3, :] = wd[a]
    taps = wdf[...]
    taps_hi = taps.astype(BF16)
    taps_lo = (taps - taps_hi.astype(F32)).astype(BF16)
    w1v[pl.ds(K1, 128), :] = jnp.concatenate(
        [taps_hi, taps_lo, jnp.zeros((96, HID), BF16)], axis=0
    )

    def dispatch(k, dx, dy, dz, dc):
        to_lat, to_lon = device(dx, dy, dz, dc)
        to = to_lat * 32 + to_lon
        src_meta, src = meta_out.at[k & 3, pl.ds(to, 1)], obs.at[pl.ds(to, 1)]
        dst_meta, dst = meta_in.at[pl.ds(k, 1)], rows_in.at[pl.ds(k, 1)]
        if isinstance(k, int) and k == 0:
            pltpu.make_async_copy(src_meta, dst_meta, mrecv.at[0]).start()
            pltpu.make_async_copy(src, dst, recv.at[0]).start()
            return
        to = (to_lat, to_lon)
        pltpu.make_async_remote_copy(
            src_ref=src_meta, dst_ref=dst_meta, send_sem=msend, recv_sem=mrecv.at[k >> 3],
            device_id=to, device_id_type=MESH,
        ).start()
        pltpu.make_async_remote_copy(
            src_ref=src, dst_ref=dst, send_sem=send, recv_sem=recv.at[k >> 3],
            device_id=to, device_id_type=MESH,
        ).start()

    pl.semaphore_wait(barrier, len(lines))
    signal(entered.at[0], y_line)
    signal(entered.at[1], z_line)
    signal(entered.at[2], z_line)
    dispatch(0, 0, 0, 0, 0)
    dispatch(1, 0, 0, 0, 1)

    def along_lines(b, carry):
        for axis in range(3):
            for dc in range(2):
                d = [0, 0, 0]
                d[axis] = b + 1
                dispatch(2 + b * 6 + axis * 2 + dc, *d, dc)
        return carry

    def along_planes(b, carry):
        for a in range(3):
            for plane in range(3):
                for dc in range(2):
                    d = [a + 1, wrapped(a + b)]
                    d.insert(2 - plane, 0)
                    dispatch(20 + b * 18 + a * 6 + plane * 2 + dc, *d, dc)
        return carry

    def elsewhere(b, carry):
        for c in range(3):
            for a in range(3):
                for dc in range(2):
                    dispatch(
                        74 + b * 18 + c * 6 + a * 2 + dc, a + 1, wrapped(a + b), wrapped(a + c), dc
                    )
        return carry

    lax.fori_loop(0, 3, along_lines, 0)
    pl.semaphore_wait(entered.at[0], 3)
    signal(entered.at[3], z_line)
    pl.semaphore_wait(entered.at[1], 3)
    pl.semaphore_wait(entered.at[2], 3)
    lax.fori_loop(0, 3, along_planes, 0)
    pl.semaphore_wait(entered.at[3], 3)
    lax.fori_loop(0, 3, elsewhere, 0)

    def spread(v):
        return jnp.broadcast_to(v.astype(F32), (16, 128)).astype(BF16)

    def codes(start, count):
        result = []
        for t in range(count // 4):
            cell = sum(meta_in[start + 4 * t + u] for u in range(4))
            alive = cell >= 0
            r = cell >> 7
            c = cell & 127
            col = (c & 1) * 64 + ((c >> 1) & 1) * 32 + (c >> 2)
            row = (r & 1) * 16 + ((r >> 1) & 1) * 8 + (r >> 2)
            pos = (
                (r & 1) * 2048 + (c & 1) * 1024 + ((r >> 1) & 1) * 512 + (r >> 2) * 64
                + ((c >> 1) & 1) * 32 + (c >> 2)
            )
            result.append(
                (
                    spread(pos & 255),
                    spread(jnp.where(alive, pos >> 8, 99)),
                    spread(pos & 127),
                    spread(jnp.where(alive, pos >> 7, 199)),
                    spread(col),
                    spread(jnp.where(alive, r - 29, 99)),
                    spread(jnp.where(alive & (c >= 125), (c - 125) * 32 + row, -1)),
                )
            )
        return result

    def across(code, which, tag, want, height):
        return jnp.concatenate(
            [one_hot(c[which], None if tag is None else c[tag], want, height) for c in code], axis=1
        )

    def dot_t(left, right):
        return lax.dot_general(left, right, (((1,), (1,)), ((), ())), preferred_element_type=F32)

    def gather_edges(code, block):
        rows = across(code, 5, None, None, 16)
        edge_dens[0:16, :] += dot_t(rows, across(code, 4, None, None, 128))
        last = across(code, 6, None, None, 128)
        edge_dens[16:32, :] += dot_t(jnp.ones_like(rows), last)
        for e in range(4):
            hot = across(code, 4, 5, e, 128) if e < 3 else last
            at = pl.ds(e * 128, 128)
            edge[at, :] += jnp.dot(hot, block, preferred_element_type=F32)

    def gather_cells(code, block):
        dens[...] += dot_t(across(code, 2, None, None, 128), across(code, 3, None, None, 128))
        for b in range(16):
            at = pl.ds(b * 256, 256)
            acc[at, :] += jnp.dot(across(code, 0, 1, b, 256), block, preferred_element_type=F32)

    def arrived(g, size):
        start = g * PER
        for u in range(size):
            one = pl.ds(start + u * PER, PER)
            pltpu.make_async_copy(meta_out.at[0, one], meta_in.at[one], mrecv.at[g + u]).wait()
            pltpu.make_async_copy(obs.at[one], rows_in.at[one], recv.at[g + u]).wait()
        count = size * PER
        return codes(start, count), rows_in[pl.ds(start, count)].reshape(count * SLOTS, CH)

    def group(g, carry):
        code, block = arrived(g * 2, 2)
        gather_edges(code, block)
        gather_cells(code, block)
        return carry

    lax.fori_loop(0, GROUPS // 2 - 1, group, 0)
    code, block = arrived(GROUPS - 2, 1)
    gather_edges(code, block)
    gather_cells(code, block)
    code, block = arrived(GROUPS - 1, 1)
    gather_edges(code, block)

    sub16 = lax.broadcasted_iota(jnp.int32, (16, 128), 0)
    amount = jnp.where(sub16 == 3, edge_dens[16:32, :], edge_dens[0:16, :])
    edge_fr_bf[...] = (amount / (1.0 + amount)).astype(BF16)
    amount = jnp.transpose(jnp.concatenate([amount, jnp.zeros((112, 128), F32)], axis=0))
    scales = 1.0 / jnp.maximum(amount, 1.0)
    fractions = amount / (1.0 + amount)
    for e in range(4):
        scale = jnp.broadcast_to(scales[:, e : e + 1], (128, 128))
        at = pl.ds(e * 128, 128)
        sums = edge[at, :]
        value = jnp.concatenate([sums[:, 0:128] * scale, sums[:, 128:CH] * scale], axis=1)
        edge[at, :] = value
        edge_bf[at, :] = value.astype(BF16)
        if e < 3:
            edge_fr[at, :] = jnp.broadcast_to(fractions[:, e : e + 1], (128, 128))
    corner[...] = jnp.zeros_like(corner)
    for a in range(3):
        for b, at in enumerate((95, 63, 127)):
            corner[pl.ds(a * 3 + b, 1), 0:CH] = edge[pl.ds(a * 128 + at, 1), :]
            corner[pl.ds(a * 3 + b, 1), CH:WIDE] = edge_fr[pl.ds(a * 128 + at, 1), :]
    corner_bf[...] = corner[...].astype(BF16)
    next_lat = (lat + 1) & 3
    next_lon = (lon + 1) & 31
    halos = [
        pltpu.make_async_remote_copy(
            src_ref=src, dst_ref=dst, send_sem=hsend.at[i], recv_sem=hrecv.at[i],
            device_id=to, device_id_type=MESH,
        )
        for i, (src, dst, to) in enumerate(
            (
                (edge_bf.at[pl.ds(0, 384)], top_in, (next_lat, lon)),
                (edge_bf.at[pl.ds(384, 96)], left_in, (lat, next_lon)),
                (corner_bf, corner_in, (next_lat, next_lon)),
                (edge_fr_bf, top_fr, (next_lat, lon)),
                (edge_fr_bf, left_fr, (lat, next_lon)),
            )
        )
    ]
    for halo in halos:
        halo.start()

    gather_cells(code, block)

    count = dens[...]
    scale_all = 1.0 / jnp.maximum(count, 1.0)
    fraction_all = count / (1.0 + count)
    for h in range(32):
        scale = jnp.broadcast_to(scale_all[:, h : h + 1], (128, 128))
        fraction = jnp.broadcast_to(fraction_all[:, h : h + 1], (128, 128))
        sums = acc[pl.ds(h * 128, 128), :]
        value = jnp.concatenate([sums[:, 0:128] * scale, sums[:, 128:CH] * scale, fraction], axis=1)
        q, p, ip, i = h >> 4, (h >> 3) & 1, (h >> 2) & 1, (h & 3) * 2
        x = x1 if q else x0
        x[p, pl.ds(offset(q, ip, i), 128), :] = value.astype(BF16)
        if p:
            for half in range(2):
                part = value[half * 64 : half * 64 + 64]
                moved = jnp.concatenate([down_one(part[32:64], jnp.zeros((1, WIDE), F32)), part[0:32]], axis=0)
                x[2, pl.ds(offset(q, ip, i + half), 64), :] = moved.astype(BF16)

    w1_copy.wait()
    lanes = lax.broadcasted_iota(jnp.int32, (16, 128), 1)
    tap_of_lane = jnp.where(lanes < 32, lanes & 15, 99).astype(F32).astype(BF16)
    bias1 = b1[...]

    def layer_one(blocks):
        shares = jnp.zeros((blocks[0].shape[0] // 16, 16, 128), BF16)
        for t, data in enumerate(blocks):
            shares = jnp.where((tap_of_lane == t)[None], data[:, CH:].reshape(-1, 16, 128), shares)
        parts = [data[:, 0:CH] for data in blocks] + [shares.reshape(-1, 128)]
        return jnp.dot(jnp.concatenate(parts, axis=1), w1v[...], preferred_element_type=F32)

    for chunk in range(4):
        ip, half = chunk >> 1, chunk & 1
        blocks = []
        for a in range(3):
            for b in range(3):
                v = (2, 0, 1)[b]
                if a == 1:
                    x, at = x0, ip * 512 + half * 256
                elif a == 2:
                    x, at = x1, ip * 576 + half * 256
                else:
                    x, at = x1, (0 if ip else 512) + half * 256
                blocks.append(x[v, pl.ds(at, 256), :])
        first = layer_one(blocks) + bias1
        if chunk == 0:
            pre_top[...] = first[0:64]
        hidden = gelu(first)
        hid = hid1 if ip else hid0
        for k in range(4):
            i = half * 4 + k
            pre_left[pl.ds(ip * 8 + i, 1), :] = first[k * 64 : k * 64 + 1]
            at = pl.ds(i * 32 + (32 if ip else 0), 32)
            odd = hidden[k * 64 + 32 : k * 64 + 64]
            hid[0, at, :] = hidden[k * 64 : k * 64 + 32].astype(BF16)
            hid[1, at, :] = odd.astype(BF16)
            hid[2, at, :] = pltpu.roll(odd, 1, 0).astype(BF16)

    for halo in halos:
        halo.wait()

    inside = jnp.where(lat > 0, 1.0, 0.0).astype(F32)

    def columns(fr):
        return jnp.transpose(jnp.concatenate([fr[...].astype(F32), jnp.zeros((112, 128), F32)], axis=0))

    top_cols = columns(top_fr)
    left_cols = columns(left_fr)
    left = jnp.concatenate(
        [left_in[...].astype(F32), jnp.broadcast_to(left_cols[0:96, 3:4], (96, 128))], axis=1
    )
    diag = corner_in[...].astype(F32) * inside
    for a in range(3):
        rows = jnp.concatenate(
            [
                top_in[pl.ds(a * 128, 128), :].astype(F32),
                jnp.broadcast_to(top_cols[:, a : a + 1], (128, 128)),
            ],
            axis=1,
        ) * inside
        p0, p1 = rows[0:64], rows[64:128]
        moved = jnp.concatenate([down_one(p1[32:64], diag[a * 3 + 2 : a * 3 + 3]), p1[0:32]], axis=0)
        for b, top in enumerate((moved, p0, p1)):
            side = left[b * 32 : b * 32 + 32]
            if a == 0:
                side = jnp.concatenate([down_one(side[24:32], diag[6 + b : 7 + b]), side[16:24]], axis=0)
            else:
                side = side[(a - 1) * 16 : a * 16]
            angle = first_row(jnp.zeros((16, WIDE), F32), diag[a * 3 + b : a * 3 + b + 1])
            xe[a * 3 + b, pl.ds(0, 64), :] = top.astype(BF16)
            xe[a * 3 + b, pl.ds(64, 16), :] = side.astype(BF16)
            xe[a * 3 + b, pl.ds(80, 16), :] = angle.astype(BF16)
    blocks = []
    for a in range(3):
        for b in range(3):
            if a == 0:
                over = xe[6 + b, pl.ds(0, 64), :]
            else:
                over = jnp.zeros((64, WIDE), BF16)
            if b == 0:
                side = xe[a * 3 + 2, pl.ds(64, 16), :]
                if a == 0:
                    side = first_row(side.astype(F32), jnp.zeros((1, WIDE), F32)).astype(BF16)
            else:
                side = jnp.zeros((16, WIDE), BF16)
            blocks.append(jnp.concatenate([xe[a * 3 + b], over, side], axis=0))
    rest = layer_one(blocks)
    ext[...] = gelu(rest[0:96] + bias1)
    above0 = ext[pl.ds(0, 32), :] * inside
    above1 = ext[pl.ds(32, 32), :] * inside
    hid1[0, pl.ds(0, 32), :] = above0.astype(BF16)
    hid1[1, pl.ds(0, 32), :] = above1.astype(BF16)
    hid1[2, pl.ds(0, 32), :] = down_one(above1, ext[pl.ds(80, 1), :] * inside).astype(BF16)
    side = rest[160:176]
    over = rest[96:160] + first_row(jnp.zeros((64, HID), F32), side[0:1])
    over = gelu(pre_top[...] + over)
    side = gelu(pre_left[...] + side)
    hid0[0, pl.ds(0, 32), :] = over[0:32].astype(BF16)
    hid0[1, pl.ds(0, 32), :] = over[32:64].astype(BF16)
    hid0[2, pl.ds(0, 32), :] = down_one(over[32:64], ext[pl.ds(64, 1), :]).astype(BF16)
    for ip in range(2):
        hid = hid1 if ip else hid0
        for i in range(8):
            n = ip * 8 + i
            if n == 0:
                continue
            at = pl.ds(i * 32 + (32 if ip else 0), 16)
            hid[0, at, :] = first_row(hid[0, at, :].astype(F32), side[n : n + 1]).astype(BF16)
            hid[2, at, :] = first_row(hid[2, at, :].astype(F32), ext[pl.ds(64 + n, 1), :]).astype(BF16)

    w2_copy.wait()
    parts = []
    for a in range(3):
        for b in range(3):
            v = (2, 0, 1)[b]
            if a == 1:
                parts.append(hid0[v])
            else:
                parts.append(hid1[v, pl.ds(32 if a == 2 else 0, 256), :])
    second = jnp.dot(jnp.concatenate(parts, axis=1), w2v[...], preferred_element_type=F32)
    out[...] = gelu(second + b2[...]).astype(BF16).reshape(8, 32, HID)

    pltpu.make_async_copy(obs.at[pl.ds(1, N - 1)], rows_in.at[pl.ds(1, N - 1)], send).wait()
    pltpu.make_async_copy(
        meta_out.at[0, pl.ds(1, N - 1)], meta_in.at[pl.ds(1, N - 1)], msend
    ).wait()


def on_device(obs, cells, counts, conv_in, conv_density, bias_in, conv_mid, bias_mid):
    vmem = pl.BlockSpec(memory_space=pltpu.VMEM)
    hbm = pl.BlockSpec(memory_space=pl.ANY)
    dma = pltpu.SemaphoreType.DMA
    return pl.pallas_call(
        kernel,
        out_shape=jax.ShapeDtypeStruct((8, 32, HID), BF16),
        in_specs=[hbm, vmem, vmem, hbm, vmem, vmem, hbm, vmem],
        out_specs=vmem,
        scratch_shapes=[
            pltpu.VMEM((N, SLOTS, CH), BF16),
            pltpu.VMEM((4, N, 1, 128), jnp.int32),
            pltpu.VMEM((N, 1, 128), jnp.int32),
            pltpu.VMEM((4096, CH), F32),
            pltpu.VMEM((128, 128), F32),
            pltpu.VMEM((512, CH), F32),
            pltpu.VMEM((512, CH), BF16),
            pltpu.VMEM((32, 128), F32),
            pltpu.VMEM((384, 128), F32),
            pltpu.VMEM((16, 128), BF16),
            pltpu.VMEM((16, WIDE), F32),
            pltpu.VMEM((16, WIDE), BF16),
            pltpu.VMEM((384, CH), BF16),
            pltpu.VMEM((96, CH), BF16),
            pltpu.VMEM((16, WIDE), BF16),
            pltpu.VMEM((16, 128), BF16),
            pltpu.VMEM((16, 128), BF16),
            pltpu.VMEM((3, 1024, WIDE), BF16),
            pltpu.VMEM((3, 1088, WIDE), BF16),
            pltpu.VMEM((9, 96, WIDE), BF16),
            pltpu.VMEM((3, 256, HID), BF16),
            pltpu.VMEM((3, 288, HID), BF16),
            pltpu.VMEM((96, HID), F32),
            pltpu.VMEM((64, HID), F32),
            pltpu.VMEM((16, HID), F32),
            pltpu.VMEM((K1 + 128, HID), BF16),
            pltpu.VMEM((K2, HID), BF16),
            pltpu.VMEM((16, HID), F32),
            pltpu.SemaphoreType.REGULAR((4,)),
            dma,
            dma((GROUPS,)),
            dma,
            dma((GROUPS,)),
            dma((2,)),
            dma((5,)),
            dma((5,)),
        ],
        compiler_params=pltpu.CompilerParams(
            collective_id=0, has_side_effects=True, vmem_limit_bytes=56 * 2**20
        ),
    )(
        obs,
        cells.T,
        counts.reshape(1, N),
        conv_in.reshape(K1, HID),
        conv_density,
        bias_in.reshape(1, HID),
        conv_mid.reshape(K2, HID),
        bias_mid.reshape(1, HID),
    )


def solution(mesh):
    return jax.shard_map(
        on_device,
        mesh=mesh,
        in_specs=(
            P(("lat", "lon"), None, None),
            P(("lat", "lon"), None),
            P(("lat", "lon")),
            P(),
            P(),
            P(),
            P(),
            P(),
        ),
        out_specs=P("lat", "lon", None),
        check_vma=False,
    )
```

```python
import functools

import jax
import jax.numpy as jnp
from jax import lax
from jax.experimental import pallas as pl
from jax.experimental.pallas import tpu as pltpu
from jax.sharding import PartitionSpec as P

MESH = pl.DeviceIdType.MESH
N = 128
SLOTS = 32
CH = 256
HID = 512
WIDE = CH + 128
PER = 8
GROUPS = N // PER
K1 = 9 * CH
K2 = 9 * HID
F32 = jnp.float32
BF16 = jnp.bfloat16


def position():
    lat = lax.axis_index("lat")
    lon = lax.axis_index("lon")
    return lon & 3, ((lat >> 1) << 1) + (lon >> 4), (lon >> 2) & 3, lat & 1


def around(v, d):
    return (v + d) & 3


def wrapped(v):
    return jnp.where(v > 2, v - 2, v + 1) if not isinstance(v, int) else v % 3 + 1


def gelu(x):
    return 0.5 * x * (1.0 + jnp.tanh(0.7978845608028654 * (x + 0.044715 * (x * x * x))))


def one_hot(ids, tag, want, height):
    if tag is not None:
        ids = jnp.where(tag == want, ids, jnp.full_like(ids, -1.0))
    rows = lax.broadcasted_iota(jnp.int32, (height, 128), 0).astype(F32).astype(BF16)
    rows = rows.reshape(height // 16, 16, 128)
    hit = rows == ids[None]
    return jnp.where(hit, jnp.ones_like(rows), jnp.zeros_like(rows)).reshape(height, 128)


def first_row(block, row):
    sub = lax.broadcasted_iota(jnp.int32, block.shape, 0)
    return jnp.where(sub == 0, jnp.broadcast_to(row, block.shape), block)


def down_one(block, row):
    return first_row(pltpu.roll(block, 1, 0), row)


def offset(q, ip, i):
    return ip * (576 if q else 512) + i * 64


def kernel(
    obs, cells_in, counts_in, w1, wd_in, b1_in, w2, hid0, hid1, w2v,
    cells, counts, wd, b1,
    rows_in, meta_out, meta_in, acc, dens, edge, edge_bf, edge_dens, edge_fr, edge_fr_bf, corner, corner_bf,
    top_in, left_in, corner_in, top_fr, left_fr,
    x0, x1, xe, ext, pre_top, pre_left, w1v, wdf,
    entered, send, recv, msend, mrecv, wsem, ssem, hsend, hrecv,
):
    small = [
        pltpu.make_async_copy(src, dst, ssem.at[i])
        for i, (src, dst) in enumerate(((cells_in, cells), (counts_in, counts), (wd_in, wd), (b1_in, b1)))
    ]
    for copy in small:
        copy.start()
    x_me, y_me, z_me, core_me = position()
    lat = lax.axis_index("lat")
    lon = lax.axis_index("lon")

    def device(dx, dy, dz, dc):
        y = around(y_me, dy)
        core = core_me ^ dc
        return (y & 2) + core, ((y & 1) << 4) + (around(z_me, dz) << 2) + around(x_me, dx)

    def signal(sem, offsets):
        for to in offsets:
            pl.semaphore_signal(sem, inc=1, device_id=device(*to), device_id_type=MESH)

    barrier = pltpu.get_barrier_semaphore()
    steps = (1, 2, 3)
    x_line = [(d, 0, 0, 0) for d in steps]
    y_line = [(0, d, 0, 0) for d in steps]
    z_line = [(0, 0, d, 0) for d in steps]
    lines = [(0, 0, 0, 1)] + [o[:3] + (c,) for o in x_line + y_line + z_line for c in (0, 1)]
    signal(barrier, lines)
    w1_copy = pltpu.make_async_copy(w1, w1v.at[pl.ds(0, K1)], wsem.at[0])
    w2_copy = pltpu.make_async_copy(w2, w2v, wsem.at[1])
    w2_copy.start()
    w1_copy.start()

    for copy in small:
        copy.wait()
    lane = lax.broadcasted_iota(jnp.int32, (N, 128), 1)
    slot = lax.broadcasted_iota(jnp.int32, (SLOTS, N), 0)
    coded = jnp.where(slot < counts[...], cells[...], -1)
    coded = jnp.transpose(jnp.concatenate([coded] * 4, axis=0))
    for v in range(4):
        meta_out[v] = jnp.where((lane >> 5) == v, coded, 0).reshape(N, 1, 128)
    acc[...] = jnp.zeros_like(acc)
    dens[...] = jnp.zeros_like(dens)
    edge[...] = jnp.zeros_like(edge)
    edge_dens[...] = jnp.zeros_like(edge_dens)
    x1[:, pl.ds(512, 64), :] = jnp.zeros((3, 64, WIDE), BF16)
    wdf[...] = jnp.zeros_like(wdf)
    for a in range(3):
        wdf[3 * a : 3 * a + 3, :] = wd[a]
    taps = wdf[...]
    taps_hi = taps.astype(BF16)
    taps_lo = (taps - taps_hi.astype(F32)).astype(BF16)
    w1v[pl.ds(K1, 128), :] = jnp.concatenate(
        [taps_hi, taps_lo, jnp.zeros((96, HID), BF16)], axis=0
    )

    def dispatch(k, dx, dy, dz, dc):
        to_lat, to_lon = device(dx, dy, dz, dc)
        to = to_lat * 32 + to_lon
        src_meta, src = meta_out.at[k & 3, pl.ds(to, 1)], obs.at[pl.ds(to, 1)]
        dst_meta, dst = meta_in.at[pl.ds(k, 1)], rows_in.at[pl.ds(k, 1)]
        if isinstance(k, int) and k == 0:
            pltpu.make_async_copy(src_meta, dst_meta, mrecv.at[0]).start()
            pltpu.make_async_copy(src, dst, recv.at[0]).start()
            return
        to = (to_lat, to_lon)
        pltpu.make_async_remote_copy(
            src_ref=src_meta, dst_ref=dst_meta, send_sem=msend, recv_sem=mrecv.at[k >> 3],
            device_id=to, device_id_type=MESH,
        ).start()
        pltpu.make_async_remote_copy(
            src_ref=src, dst_ref=dst, send_sem=send, recv_sem=recv.at[k >> 3],
            device_id=to, device_id_type=MESH,
        ).start()

    pl.semaphore_wait(barrier, len(lines))
    signal(entered.at[0], y_line)
    signal(entered.at[1], z_line)
    signal(entered.at[2], z_line)
    dispatch(0, 0, 0, 0, 0)
    dispatch(1, 0, 0, 0, 1)

    def along_lines(b, carry):
        for axis in range(3):
            for dc in range(2):
                d = [0, 0, 0]
                d[axis] = b + 1
                dispatch(2 + b * 6 + axis * 2 + dc, *d, dc)
        return carry

    def along_planes(b, carry):
        for dc in range(2):
            for a in range(3):
                for plane in range(3):
                    d = [a + 1, wrapped(a + b)]
                    d.insert(2 - plane, 0)
                    dispatch(20 + b * 18 + a * 6 + plane * 2 + dc, *d, dc)
        return carry

    def elsewhere(b, carry):
        for dc in range(2):
            for c in range(3):
                for a in range(3):
                    dispatch(
                        74 + b * 18 + c * 6 + a * 2 + dc, a + 1, wrapped(a + b), wrapped(a + c), dc
                    )
        return carry

    lax.fori_loop(0, 3, along_lines, 0)
    pl.semaphore_wait(entered.at[0], 3)
    signal(entered.at[3], z_line)
    pl.semaphore_wait(entered.at[1], 3)
    pl.semaphore_wait(entered.at[2], 3)
    lax.fori_loop(0, 3, along_planes, 0)
    pl.semaphore_wait(entered.at[3], 3)
    lax.fori_loop(0, 3, elsewhere, 0)

    def spread(v):
        return jnp.broadcast_to(v.astype(F32), (16, 128)).astype(BF16)

    def codes(start, count):
        result = []
        for t in range(count // 4):
            cell = sum(meta_in[start + 4 * t + u] for u in range(4))
            alive = cell >= 0
            r = cell >> 7
            c = cell & 127
            col = (c & 1) * 64 + ((c >> 1) & 1) * 32 + (c >> 2)
            row = (r & 1) * 16 + ((r >> 1) & 1) * 8 + (r >> 2)
            pos = (
                (r & 1) * 2048 + (c & 1) * 1024 + ((r >> 1) & 1) * 512 + (r >> 2) * 64
                + ((c >> 1) & 1) * 32 + (c >> 2)
            )
            result.append(
                (
                    spread(pos & 255),
                    spread(jnp.where(alive, pos >> 8, 99)),
                    spread(pos & 127),
                    spread(jnp.where(alive, pos >> 7, 199)),
                    spread(col),
                    spread(jnp.where(alive, r - 29, 99)),
                    spread(jnp.where(alive & (c >= 125), (c - 125) * 32 + row, -1)),
                )
            )
        return result

    def across(code, which, tag, want, height):
        return jnp.concatenate(
            [one_hot(c[which], None if tag is None else c[tag], want, height) for c in code], axis=1
        )

    def dot_t(left, right):
        return lax.dot_general(left, right, (((1,), (1,)), ((), ())), preferred_element_type=F32)

    def gather_edges(code, block):
        rows = across(code, 5, None, None, 16)
        edge_dens[0:16, :] += dot_t(rows, across(code, 4, None, None, 128))
        last = across(code, 6, None, None, 128)
        edge_dens[16:32, :] += dot_t(jnp.ones_like(rows), last)
        for e in range(4):
            hot = across(code, 4, 5, e, 128) if e < 3 else last
            at = pl.ds(e * 128, 128)
            edge[at, :] += jnp.dot(hot, block, preferred_element_type=F32)

    def gather_cells(code, block):
        dens[...] += dot_t(across(code, 2, None, None, 128), across(code, 3, None, None, 128))
        for b in range(16):
            at = pl.ds(b * 256, 256)
            acc[at, :] += jnp.dot(across(code, 0, 1, b, 256), block, preferred_element_type=F32)

    def arrived(g, size):
        start = g * PER
        for u in range(size):
            one = pl.ds(start + u * PER, PER)
            pltpu.make_async_copy(meta_out.at[0, one], meta_in.at[one], mrecv.at[g + u]).wait()
            pltpu.make_async_copy(obs.at[one], rows_in.at[one], recv.at[g + u]).wait()
        count = size * PER
        return codes(start, count), rows_in[pl.ds(start, count)].reshape(count * SLOTS, CH)

    def group(g, carry):
        code, block = arrived(g * 2, 2)
        gather_edges(code, block)
        gather_cells(code, block)
        return carry

    lax.fori_loop(0, GROUPS // 2 - 1, group, 0)
    code, block = arrived(GROUPS - 2, 1)
    gather_edges(code, block)
    gather_cells(code, block)
    code, block = arrived(GROUPS - 1, 1)
    gather_edges(code, block)

    sub16 = lax.broadcasted_iota(jnp.int32, (16, 128), 0)
    amount = jnp.where(sub16 == 3, edge_dens[16:32, :], edge_dens[0:16, :])
    edge_fr_bf[...] = (amount / (1.0 + amount)).astype(BF16)
    amount = jnp.transpose(jnp.concatenate([amount, jnp.zeros((112, 128), F32)], axis=0))
    scales = 1.0 / jnp.maximum(amount, 1.0)
    fractions = amount / (1.0 + amount)
    for e in range(4):
        scale = jnp.broadcast_to(scales[:, e : e + 1], (128, 128))
        at = pl.ds(e * 128, 128)
        sums = edge[at, :]
        value = jnp.concatenate([sums[:, 0:128] * scale, sums[:, 128:CH] * scale], axis=1)
        edge[at, :] = value
        edge_bf[at, :] = value.astype(BF16)
        if e < 3:
            edge_fr[at, :] = jnp.broadcast_to(fractions[:, e : e + 1], (128, 128))
    corner[...] = jnp.zeros_like(corner)
    for a in range(3):
        for b, at in enumerate((95, 63, 127)):
            corner[pl.ds(a * 3 + b, 1), 0:CH] = edge[pl.ds(a * 128 + at, 1), :]
            corner[pl.ds(a * 3 + b, 1), CH:WIDE] = edge_fr[pl.ds(a * 128 + at, 1), :]
    corner_bf[...] = corner[...].astype(BF16)
    next_lat = (lat + 1) & 3
    next_lon = (lon + 1) & 31
    halos = [
        pltpu.make_async_remote_copy(
            src_ref=src, dst_ref=dst, send_sem=hsend.at[i], recv_sem=hrecv.at[i],
            device_id=to, device_id_type=MESH,
        )
        for i, (src, dst, to) in enumerate(
            (
                (edge_bf.at[pl.ds(0, 384)], top_in, (next_lat, lon)),
                (edge_bf.at[pl.ds(384, 96)], left_in, (lat, next_lon)),
                (corner_bf, corner_in, (next_lat, next_lon)),
                (edge_fr_bf, top_fr, (next_lat, lon)),
                (edge_fr_bf, left_fr, (lat, next_lon)),
            )
        )
    ]
    for halo in halos:
        halo.start()

    gather_cells(code, block)

    count = dens[...]
    scale_all = 1.0 / jnp.maximum(count, 1.0)
    fraction_all = count / (1.0 + count)
    for h in range(32):
        scale = jnp.broadcast_to(scale_all[:, h : h + 1], (128, 128))
        fraction = jnp.broadcast_to(fraction_all[:, h : h + 1], (128, 128))
        sums = acc[pl.ds(h * 128, 128), :]
        value = jnp.concatenate([sums[:, 0:128] * scale, sums[:, 128:CH] * scale, fraction], axis=1)
        q, p, ip, i = h >> 4, (h >> 3) & 1, (h >> 2) & 1, (h & 3) * 2
        x = x1 if q else x0
        x[p, pl.ds(offset(q, ip, i), 128), :] = value.astype(BF16)
        if p:
            for half in range(2):
                part = value[half * 64 : half * 64 + 64]
                moved = jnp.concatenate([down_one(part[32:64], jnp.zeros((1, WIDE), F32)), part[0:32]], axis=0)
                x[2, pl.ds(offset(q, ip, i + half), 64), :] = moved.astype(BF16)

    w1_copy.wait()
    lanes = lax.broadcasted_iota(jnp.int32, (16, 128), 1)
    tap_of_lane = jnp.where(lanes < 32, lanes & 15, 99).astype(F32).astype(BF16)
    bias1 = b1[...]

    def layer_one(blocks):
        shares = jnp.zeros((blocks[0].shape[0] // 16, 16, 128), BF16)
        for t, data in enumerate(blocks):
            shares = jnp.where((tap_of_lane == t)[None], data[:, CH:].reshape(-1, 16, 128), shares)
        parts = [data[:, 0:CH] for data in blocks] + [shares.reshape(-1, 128)]
        return jnp.dot(jnp.concatenate(parts, axis=1), w1v[...], preferred_element_type=F32)

    for chunk in range(4):
        ip, half = chunk >> 1, chunk & 1
        blocks = []
        for a in range(3):
            for b in range(3):
                v = (2, 0, 1)[b]
                if a == 1:
                    x, at = x0, ip * 512 + half * 256
                elif a == 2:
                    x, at = x1, ip * 576 + half * 256
                else:
                    x, at = x1, (0 if ip else 512) + half * 256
                blocks.append(x[v, pl.ds(at, 256), :])
        first = layer_one(blocks) + bias1
        if chunk == 0:
            pre_top[...] = first[0:64]
        hidden = gelu(first)
        hid = hid1 if ip else hid0
        for k in range(4):
            i = half * 4 + k
            pre_left[pl.ds(ip * 8 + i, 1), :] = first[k * 64 : k * 64 + 1]
            at = pl.ds(i * 32 + (32 if ip else 0), 32)
            odd = hidden[k * 64 + 32 : k * 64 + 64]
            hid[0, at, :] = hidden[k * 64 : k * 64 + 32].astype(BF16)
            hid[1, at, :] = odd.astype(BF16)
            hid[2, at, :] = pltpu.roll(odd, 1, 0).astype(BF16)

    for halo in halos:
        halo.wait()

    inside = jnp.where(lat > 0, 1.0, 0.0).astype(F32)

    def columns(fr):
        return jnp.transpose(jnp.concatenate([fr[...].astype(F32), jnp.zeros((112, 128), F32)], axis=0))

    top_cols = columns(top_fr)
    left_cols = columns(left_fr)
    left = jnp.concatenate(
        [left_in[...].astype(F32), jnp.broadcast_to(left_cols[0:96, 3:4], (96, 128))], axis=1
    )
    diag = corner_in[...].astype(F32) * inside
    for a in range(3):
        rows = jnp.concatenate(
            [
                top_in[pl.ds(a * 128, 128), :].astype(F32),
                jnp.broadcast_to(top_cols[:, a : a + 1], (128, 128)),
            ],
            axis=1,
        ) * inside
        p0, p1 = rows[0:64], rows[64:128]
        moved = jnp.concatenate([down_one(p1[32:64], diag[a * 3 + 2 : a * 3 + 3]), p1[0:32]], axis=0)
        for b, top in enumerate((moved, p0, p1)):
            side = left[b * 32 : b * 32 + 32]
            if a == 0:
                side = jnp.concatenate([down_one(side[24:32], diag[6 + b : 7 + b]), side[16:24]], axis=0)
            else:
                side = side[(a - 1) * 16 : a * 16]
            angle = first_row(jnp.zeros((16, WIDE), F32), diag[a * 3 + b : a * 3 + b + 1])
            xe[a * 3 + b, pl.ds(0, 64), :] = top.astype(BF16)
            xe[a * 3 + b, pl.ds(64, 16), :] = side.astype(BF16)
            xe[a * 3 + b, pl.ds(80, 16), :] = angle.astype(BF16)
    blocks = []
    for a in range(3):
        for b in range(3):
            if a == 0:
                over = xe[6 + b, pl.ds(0, 64), :]
            else:
                over = jnp.zeros((64, WIDE), BF16)
            if b == 0:
                side = xe[a * 3 + 2, pl.ds(64, 16), :]
                if a == 0:
                    side = first_row(side.astype(F32), jnp.zeros((1, WIDE), F32)).astype(BF16)
            else:
                side = jnp.zeros((16, WIDE), BF16)
            blocks.append(jnp.concatenate([xe[a * 3 + b], over, side], axis=0))
    rest = layer_one(blocks)
    ext[...] = gelu(rest[0:96] + bias1)
    above0 = ext[pl.ds(0, 32), :] * inside
    above1 = ext[pl.ds(32, 32), :] * inside
    hid1[0, pl.ds(0, 32), :] = above0.astype(BF16)
    hid1[1, pl.ds(0, 32), :] = above1.astype(BF16)
    hid1[2, pl.ds(0, 32), :] = down_one(above1, ext[pl.ds(80, 1), :] * inside).astype(BF16)
    side = rest[160:176]
    over = rest[96:160] + first_row(jnp.zeros((64, HID), F32), side[0:1])
    over = gelu(pre_top[...] + over)
    side = gelu(pre_left[...] + side)
    hid0[0, pl.ds(0, 32), :] = over[0:32].astype(BF16)
    hid0[1, pl.ds(0, 32), :] = over[32:64].astype(BF16)
    hid0[2, pl.ds(0, 32), :] = down_one(over[32:64], ext[pl.ds(64, 1), :]).astype(BF16)
    for ip in range(2):
        hid = hid1 if ip else hid0
        for i in range(8):
            n = ip * 8 + i
            if n == 0:
                continue
            at = pl.ds(i * 32 + (32 if ip else 0), 16)
            hid[0, at, :] = first_row(hid[0, at, :].astype(F32), side[n : n + 1]).astype(BF16)
            hid[2, at, :] = first_row(hid[2, at, :].astype(F32), ext[pl.ds(64 + n, 1), :]).astype(BF16)

    w2_copy.wait()
    pltpu.make_async_copy(obs.at[pl.ds(1, N - 1)], rows_in.at[pl.ds(1, N - 1)], send).wait()
    pltpu.make_async_copy(
        meta_out.at[0, pl.ds(1, N - 1)], meta_in.at[pl.ds(1, N - 1)], msend
    ).wait()


def layer_two(hid0, hid1, w2, b2, out):
    parts = []
    for a in range(3):
        for b in range(3):
            v = (2, 0, 1)[b]
            if a == 1:
                parts.append(hid0[v])
            else:
                parts.append(hid1[v, pl.ds(32 if a == 2 else 0, 256), :])
    second = jnp.dot(jnp.concatenate(parts, axis=1), w2[...], preferred_element_type=F32)
    out[...] = gelu(second + b2[...]).astype(BF16).reshape(8, 32, HID)


def on_device(obs, cells, counts, conv_in, conv_density, bias_in, conv_mid, bias_mid):
    vmem = pl.BlockSpec(memory_space=pltpu.VMEM)
    hbm = pl.BlockSpec(memory_space=pltpu.HBM)
    dma = pltpu.SemaphoreType.DMA
    hid0, hid1, w2 = pl.pallas_call(
        kernel,
        out_shape=[
            pltpu.VMEM((3, 256, HID), BF16),
            pltpu.VMEM((3, 288, HID), BF16),
            pltpu.VMEM((K2, HID), BF16),
        ],
        in_specs=[hbm] * 7,
        out_specs=[vmem, vmem, vmem],
        scratch_shapes=[
            pltpu.VMEM((SLOTS, N), jnp.int32),
            pltpu.VMEM((1, N), jnp.int32),
            pltpu.VMEM((3, 3, HID), F32),
            pltpu.VMEM((1, HID), F32),
            pltpu.VMEM((N, SLOTS, CH), BF16),
            pltpu.VMEM((4, N, 1, 128), jnp.int32),
            pltpu.VMEM((N, 1, 128), jnp.int32),
            pltpu.VMEM((4096, CH), F32),
            pltpu.VMEM((128, 128), F32),
            pltpu.VMEM((512, CH), F32),
            pltpu.VMEM((512, CH), BF16),
            pltpu.VMEM((32, 128), F32),
            pltpu.VMEM((384, 128), F32),
            pltpu.VMEM((16, 128), BF16),
            pltpu.VMEM((16, WIDE), F32),
            pltpu.VMEM((16, WIDE), BF16),
            pltpu.VMEM((384, CH), BF16),
            pltpu.VMEM((96, CH), BF16),
            pltpu.VMEM((16, WIDE), BF16),
            pltpu.VMEM((16, 128), BF16),
            pltpu.VMEM((16, 128), BF16),
            pltpu.VMEM((3, 1024, WIDE), BF16),
            pltpu.VMEM((3, 1088, WIDE), BF16),
            pltpu.VMEM((9, 96, WIDE), BF16),
            pltpu.VMEM((96, HID), F32),
            pltpu.VMEM((64, HID), F32),
            pltpu.VMEM((16, HID), F32),
            pltpu.VMEM((K1 + 128, HID), BF16),
            pltpu.VMEM((16, HID), F32),
            pltpu.SemaphoreType.REGULAR((4,)),
            dma,
            dma((GROUPS,)),
            dma,
            dma((GROUPS,)),
            dma((2,)),
            dma((4,)),
            dma((5,)),
            dma((5,)),
        ],
        compiler_params=pltpu.CompilerParams(
            collective_id=0, has_side_effects=True, vmem_limit_bytes=54 * 2**20
        ),
    )(
        obs,
        cells.T,
        counts.reshape(1, N),
        conv_in.reshape(K1, HID),
        conv_density,
        bias_in.reshape(1, HID),
        conv_mid.reshape(K2, HID),
    )
    return pl.pallas_call(
        layer_two,
        out_shape=jax.ShapeDtypeStruct((8, 32, HID), BF16),
        in_specs=[vmem, vmem, vmem, vmem],
        out_specs=vmem,
        compiler_params=pltpu.CompilerParams(vmem_limit_bytes=20 * 2**20),
    )(hid0, hid1, w2, bias_mid.reshape(1, HID))


def solution(mesh):
    return jax.shard_map(
        on_device,
        mesh=mesh,
        in_specs=(
            P(("lat", "lon"), None, None),
            P(("lat", "lon"), None),
            P(("lat", "lon")),
            P(),
            P(),
            P(),
            P(),
            P(),
        ),
        out_specs=P("lat", "lon", None),
        check_vma=False,
    )
```

```python
import functools

import jax
import jax.numpy as jnp
from jax import lax
from jax.experimental import pallas as pl
from jax.experimental.pallas import tpu as pltpu
from jax.sharding import PartitionSpec as P

MESH = pl.DeviceIdType.MESH
N = 128
SLOTS = 32
CH = 256
HID = 512
WIDE = CH + 128
PER = 8
GROUPS = N // PER
K1 = 9 * CH
K2 = 9 * HID
F32 = jnp.float32
BF16 = jnp.bfloat16


def position():
    lat = lax.axis_index("lat")
    lon = lax.axis_index("lon")
    return lon & 3, ((lat >> 1) << 1) + (lon >> 4), (lon >> 2) & 3, lat & 1


def around(v, d):
    return (v + d) & 3


def wrapped(v):
    return jnp.where(v > 2, v - 2, v + 1) if not isinstance(v, int) else v % 3 + 1


def gelu(x):
    return 0.5 * x * (1.0 + jnp.tanh(0.7978845608028654 * (x + 0.044715 * (x * x * x))))


def one_hot(ids, tag, want, height):
    if tag is not None:
        ids = jnp.where(tag == want, ids, jnp.full_like(ids, -1.0))
    rows = lax.broadcasted_iota(jnp.int32, (height, 128), 0).astype(F32).astype(BF16)
    rows = rows.reshape(height // 16, 16, 128)
    hit = rows == ids[None]
    return jnp.where(hit, jnp.ones_like(rows), jnp.zeros_like(rows)).reshape(height, 128)


def first_row(block, row):
    sub = lax.broadcasted_iota(jnp.int32, block.shape, 0)
    return jnp.where(sub == 0, jnp.broadcast_to(row, block.shape), block)


def down_one(block, row):
    return first_row(pltpu.roll(block, 1, 0), row)


def offset(q, ip, i):
    return ip * (576 if q else 512) + i * 64


def kernel(
    obs, cells_in, counts_in, w1, wd_in, b1_in, w2, hid0, hid1, w2v,
    cells, counts, wd, b1,
    rows_in, meta_out, meta_in, acc, dens, edge, edge_bf, edge_dens, edge_fr, edge_fr_bf, corner, corner_bf,
    top_in, left_in, corner_in, top_fr, left_fr,
    x0, x1, xe, ext, pre_top, pre_left, w1v, wdf,
    entered, send, recv, msend, mrecv, wsem, ssem, hsend, hrecv,
):
    small = [
        pltpu.make_async_copy(src, dst, ssem.at[i])
        for i, (src, dst) in enumerate(((cells_in, cells), (counts_in, counts), (wd_in, wd), (b1_in, b1)))
    ]
    for copy in small:
        copy.start()
    x_me, y_me, z_me, core_me = position()
    lat = lax.axis_index("lat")
    lon = lax.axis_index("lon")

    def device(dx, dy, dz, dc):
        y = around(y_me, dy)
        core = core_me ^ dc
        return (y & 2) + core, ((y & 1) << 4) + (around(z_me, dz) << 2) + around(x_me, dx)

    def signal(sem, offsets):
        for to in offsets:
            pl.semaphore_signal(sem, inc=1, device_id=device(*to), device_id_type=MESH)

    barrier = pltpu.get_barrier_semaphore()
    steps = (1, 2, 3)
    x_line = [(d, 0, 0, 0) for d in steps]
    y_line = [(0, d, 0, 0) for d in steps]
    z_line = [(0, 0, d, 0) for d in steps]
    lines = [(0, 0, 0, 1)] + [o[:3] + (c,) for o in x_line + y_line + z_line for c in (0, 1)]
    signal(barrier, lines)
    w1_copy = pltpu.make_async_copy(w1, w1v.at[pl.ds(0, K1)], wsem.at[0])
    w2_copy = pltpu.make_async_copy(w2, w2v, wsem.at[1])
    w2_copy.start()
    w1_copy.start()

    for copy in small:
        copy.wait()
    lane = lax.broadcasted_iota(jnp.int32, (N, 128), 1)
    slot = lax.broadcasted_iota(jnp.int32, (SLOTS, N), 0)
    coded = jnp.where(slot < counts[...], cells[...], -1)
    coded = jnp.transpose(jnp.concatenate([coded] * 4, axis=0))
    for v in range(4):
        meta_out[v] = jnp.where((lane >> 5) == v, coded, 0).reshape(N, 1, 128)

    @pl.when(lat == 0)
    def _():
        for ref in (top_in, corner_in, top_fr):
            ref[...] = jnp.zeros_like(ref)

    acc[...] = jnp.zeros_like(acc)
    dens[...] = jnp.zeros_like(dens)
    edge[...] = jnp.zeros_like(edge)
    edge_dens[...] = jnp.zeros_like(edge_dens)
    x1[:, pl.ds(512, 64), :] = jnp.zeros((3, 64, WIDE), BF16)
    wdf[...] = jnp.zeros_like(wdf)
    for a in range(3):
        wdf[3 * a : 3 * a + 3, :] = wd[a]
    taps = wdf[...]
    taps_hi = taps.astype(BF16)
    taps_lo = (taps - taps_hi.astype(F32)).astype(BF16)
    w1v[pl.ds(K1, 128), :] = jnp.concatenate(
        [taps_hi, taps_lo, jnp.zeros((96, HID), BF16)], axis=0
    )

    def dispatch(k, dx, dy, dz, dc):
        to_lat, to_lon = device(dx, dy, dz, dc)
        to = to_lat * 32 + to_lon
        src_meta, src = meta_out.at[k & 3, pl.ds(to, 1)], obs.at[pl.ds(to, 1)]
        dst_meta, dst = meta_in.at[pl.ds(k, 1)], rows_in.at[pl.ds(k, 1)]
        if isinstance(k, int) and k == 0:
            pltpu.make_async_copy(src_meta, dst_meta, mrecv.at[0]).start()
            pltpu.make_async_copy(src, dst, recv.at[0]).start()
            return
        to = (to_lat, to_lon)
        pltpu.make_async_remote_copy(
            src_ref=src_meta, dst_ref=dst_meta, send_sem=msend, recv_sem=mrecv.at[k >> 3],
            device_id=to, device_id_type=MESH,
        ).start()
        pltpu.make_async_remote_copy(
            src_ref=src, dst_ref=dst, send_sem=send, recv_sem=recv.at[k >> 3],
            device_id=to, device_id_type=MESH,
        ).start()

    pl.semaphore_wait(barrier, len(lines))
    signal(entered.at[0], y_line)
    signal(entered.at[1], z_line)
    signal(entered.at[2], z_line)
    dispatch(0, 0, 0, 0, 0)
    dispatch(1, 0, 0, 0, 1)

    def along_lines(b, carry):
        for axis in range(3):
            for dc in range(2):
                d = [0, 0, 0]
                d[axis] = b + 1
                dispatch(2 + b * 6 + axis * 2 + dc, *d, dc)
        return carry

    def along_planes(b, carry):
        for dc in range(2):
            for a in range(3):
                for plane in range(3):
                    d = [a + 1, wrapped(a + b)]
                    d.insert(2 - plane, 0)
                    dispatch(20 + b * 18 + a * 6 + plane * 2 + dc, *d, dc)
        return carry

    def elsewhere(b, carry):
        for dc in range(2):
            for c in range(3):
                for a in range(3):
                    dispatch(
                        74 + b * 18 + c * 6 + a * 2 + dc, a + 1, wrapped(a + b), wrapped(a + c), dc
                    )
        return carry

    lax.fori_loop(0, 3, along_lines, 0)
    pl.semaphore_wait(entered.at[0], 3)
    signal(entered.at[3], z_line)
    pl.semaphore_wait(entered.at[1], 3)
    pl.semaphore_wait(entered.at[2], 3)
    lax.fori_loop(0, 3, along_planes, 0)
    pl.semaphore_wait(entered.at[3], 3)
    lax.fori_loop(0, 3, elsewhere, 0)

    def spread(v):
        return jnp.broadcast_to(v.astype(F32), (16, 128)).astype(BF16)

    def codes(start, count):
        result = []
        for t in range(count // 4):
            cell = sum(meta_in[start + 4 * t + u] for u in range(4))
            alive = cell >= 0
            r = cell >> 7
            c = cell & 127
            col = (c & 1) * 64 + ((c >> 1) & 1) * 32 + (c >> 2)
            row = (r & 1) * 16 + ((r >> 1) & 1) * 8 + (r >> 2)
            pos = (
                (r & 1) * 2048 + (c & 1) * 1024 + ((r >> 1) & 1) * 512 + (r >> 2) * 64
                + ((c >> 1) & 1) * 32 + (c >> 2)
            )
            result.append(
                (
                    spread(pos & 255),
                    spread(jnp.where(alive, pos >> 8, 99)),
                    spread(pos & 127),
                    spread(jnp.where(alive, pos >> 7, 199)),
                    spread(col),
                    spread(jnp.where(alive, r - 29, 99)),
                    spread(jnp.where(alive & (c >= 125), (c - 125) * 32 + row, -1)),
                )
            )
        return result

    def across(code, which, tag, want, height):
        return jnp.concatenate(
            [one_hot(c[which], None if tag is None else c[tag], want, height) for c in code], axis=1
        )

    def dot_t(left, right):
        return lax.dot_general(left, right, (((1,), (1,)), ((), ())), preferred_element_type=F32)

    def gather_edges(code, block):
        rows = across(code, 5, None, None, 16)
        edge_dens[0:16, :] += dot_t(rows, across(code, 4, None, None, 128))
        last = across(code, 6, None, None, 128)
        edge_dens[16:32, :] += dot_t(jnp.ones_like(rows), last)
        for e in range(4):
            hot = across(code, 4, 5, e, 128) if e < 3 else last
            at = pl.ds(e * 128, 128)
            edge[at, :] += jnp.dot(hot, block, preferred_element_type=F32)

    def gather_cells(code, block):
        dens[...] += dot_t(across(code, 2, None, None, 128), across(code, 3, None, None, 128))
        for b in range(16):
            at = pl.ds(b * 256, 256)
            acc[at, :] += jnp.dot(across(code, 0, 1, b, 256), block, preferred_element_type=F32)

    def arrived(g, size):
        start = g * PER
        for u in range(size):
            one = pl.ds(start + u * PER, PER)
            pltpu.make_async_copy(meta_out.at[0, one], meta_in.at[one], mrecv.at[g + u]).wait()
            pltpu.make_async_copy(obs.at[one], rows_in.at[one], recv.at[g + u]).wait()
        count = size * PER
        return codes(start, count), rows_in[pl.ds(start, count)].reshape(count * SLOTS, CH)

    def group(g, carry):
        code, block = arrived(g * 2, 2)
        gather_edges(code, block)
        gather_cells(code, block)
        return carry

    lax.fori_loop(0, GROUPS // 2 - 1, group, 0)
    code, block = arrived(GROUPS - 2, 1)
    gather_edges(code, block)
    gather_cells(code, block)
    code, block = arrived(GROUPS - 1, 1)
    gather_edges(code, block)

    sub16 = lax.broadcasted_iota(jnp.int32, (16, 128), 0)
    amount = jnp.where(sub16 == 3, edge_dens[16:32, :], edge_dens[0:16, :])
    edge_fr_bf[...] = (amount / (1.0 + amount)).astype(BF16)
    amount = jnp.transpose(jnp.concatenate([amount, jnp.zeros((112, 128), F32)], axis=0))
    scales = 1.0 / jnp.maximum(amount, 1.0)
    fractions = amount / (1.0 + amount)
    for e in range(4):
        scale = jnp.broadcast_to(scales[:, e : e + 1], (128, 128))
        at = pl.ds(e * 128, 128)
        sums = edge[at, :]
        value = jnp.concatenate([sums[:, 0:128] * scale, sums[:, 128:CH] * scale], axis=1)
        edge[at, :] = value
        edge_bf[at, :] = value.astype(BF16)
        if e < 3:
            edge_fr[at, :] = jnp.broadcast_to(fractions[:, e : e + 1], (128, 128))
    corner[...] = jnp.zeros_like(corner)
    for a in range(3):
        for b, at in enumerate((95, 63, 127)):
            corner[pl.ds(a * 3 + b, 1), 0:CH] = edge[pl.ds(a * 128 + at, 1), :]
            corner[pl.ds(a * 3 + b, 1), CH:WIDE] = edge_fr[pl.ds(a * 128 + at, 1), :]
    corner_bf[...] = corner[...].astype(BF16)
    next_lat = (lat + 1) & 3
    next_lon = (lon + 1) & 31
    halos = [
        pltpu.make_async_remote_copy(
            src_ref=src, dst_ref=dst, send_sem=hsend.at[i], recv_sem=hrecv.at[i],
            device_id=to, device_id_type=MESH,
        )
        for i, (src, dst, to) in enumerate(
            (
                (edge_bf.at[pl.ds(0, 384)], top_in, (next_lat, lon)),
                (edge_bf.at[pl.ds(384, 96)], left_in, (lat, next_lon)),
                (corner_bf, corner_in, (next_lat, next_lon)),
                (edge_fr_bf, top_fr, (next_lat, lon)),
                (edge_fr_bf, left_fr, (lat, next_lon)),
            )
        )
    ]
    tops, lefts = (halos[0], halos[2], halos[3]), (halos[1], halos[4])
    for halo in lefts:
        halo.start()

    @pl.when(lat < 3)
    def _():
        for halo in tops:
            halo.start()

    gather_cells(code, block)

    count = dens[...]
    scale_all = 1.0 / jnp.maximum(count, 1.0)
    fraction_all = count / (1.0 + count)
    for h in range(32):
        scale = jnp.broadcast_to(scale_all[:, h : h + 1], (128, 128))
        fraction = jnp.broadcast_to(fraction_all[:, h : h + 1], (128, 128))
        sums = acc[pl.ds(h * 128, 128), :]
        value = jnp.concatenate([sums[:, 0:128] * scale, sums[:, 128:CH] * scale, fraction], axis=1)
        q, p, ip, i = h >> 4, (h >> 3) & 1, (h >> 2) & 1, (h & 3) * 2
        x = x1 if q else x0
        x[p, pl.ds(offset(q, ip, i), 128), :] = value.astype(BF16)
        if p:
            for half in range(2):
                part = value[half * 64 : half * 64 + 64]
                moved = jnp.concatenate([down_one(part[32:64], jnp.zeros((1, WIDE), F32)), part[0:32]], axis=0)
                x[2, pl.ds(offset(q, ip, i + half), 64), :] = moved.astype(BF16)

    w1_copy.wait()
    lanes = lax.broadcasted_iota(jnp.int32, (16, 128), 1)
    tap_of_lane = jnp.where(lanes < 32, lanes & 15, 99).astype(F32).astype(BF16)
    bias1 = b1[...]

    def layer_one(blocks):
        shares = jnp.zeros((blocks[0].shape[0] // 16, 16, 128), BF16)
        for t, data in enumerate(blocks):
            shares = jnp.where((tap_of_lane == t)[None], data[:, CH:].reshape(-1, 16, 128), shares)
        parts = [data[:, 0:CH] for data in blocks] + [shares.reshape(-1, 128)]
        return jnp.dot(jnp.concatenate(parts, axis=1), w1v[...], preferred_element_type=F32)

    for chunk in range(4):
        ip, half = chunk >> 1, chunk & 1
        blocks = []
        for a in range(3):
            for b in range(3):
                v = (2, 0, 1)[b]
                if a == 1:
                    x, at = x0, ip * 512 + half * 256
                elif a == 2:
                    x, at = x1, ip * 576 + half * 256
                else:
                    x, at = x1, (0 if ip else 512) + half * 256
                blocks.append(x[v, pl.ds(at, 256), :])
        first = layer_one(blocks) + bias1
        if chunk == 0:
            pre_top[...] = first[0:64]
        hidden = gelu(first)
        hid = hid1 if ip else hid0
        for k in range(4):
            i = half * 4 + k
            pre_left[pl.ds(ip * 8 + i, 1), :] = first[k * 64 : k * 64 + 1]
            at = pl.ds(i * 32 + (32 if ip else 0), 32)
            odd = hidden[k * 64 + 32 : k * 64 + 64]
            hid[0, at, :] = hidden[k * 64 : k * 64 + 32].astype(BF16)
            hid[1, at, :] = odd.astype(BF16)
            hid[2, at, :] = pltpu.roll(odd, 1, 0).astype(BF16)

    for halo in lefts:
        halo.wait()

    @pl.when(lat < 3)
    def _():
        for halo in tops:
            halo.wait_send()

    @pl.when(lat > 0)
    def _():
        for halo in tops:
            halo.wait_recv()

    inside = jnp.where(lat > 0, 1.0, 0.0).astype(F32)

    def columns(fr):
        return jnp.transpose(jnp.concatenate([fr[...].astype(F32), jnp.zeros((112, 128), F32)], axis=0))

    top_cols = columns(top_fr)
    left_cols = columns(left_fr)
    left = jnp.concatenate(
        [left_in[...].astype(F32), jnp.broadcast_to(left_cols[0:96, 3:4], (96, 128))], axis=1
    )
    diag = corner_in[...].astype(F32) * inside
    for a in range(3):
        rows = jnp.concatenate(
            [
                top_in[pl.ds(a * 128, 128), :].astype(F32),
                jnp.broadcast_to(top_cols[:, a : a + 1], (128, 128)),
            ],
            axis=1,
        ) * inside
        p0, p1 = rows[0:64], rows[64:128]
        moved = jnp.concatenate([down_one(p1[32:64], diag[a * 3 + 2 : a * 3 + 3]), p1[0:32]], axis=0)
        for b, top in enumerate((moved, p0, p1)):
            side = left[b * 32 : b * 32 + 32]
            if a == 0:
                side = jnp.concatenate([down_one(side[24:32], diag[6 + b : 7 + b]), side[16:24]], axis=0)
            else:
                side = side[(a - 1) * 16 : a * 16]
            angle = first_row(jnp.zeros((16, WIDE), F32), diag[a * 3 + b : a * 3 + b + 1])
            xe[a * 3 + b, pl.ds(0, 64), :] = top.astype(BF16)
            xe[a * 3 + b, pl.ds(64, 16), :] = side.astype(BF16)
            xe[a * 3 + b, pl.ds(80, 16), :] = angle.astype(BF16)
    blocks = []
    for a in range(3):
        for b in range(3):
            if a == 0:
                over = xe[6 + b, pl.ds(0, 64), :]
            else:
                over = jnp.zeros((64, WIDE), BF16)
            if b == 0:
                side = xe[a * 3 + 2, pl.ds(64, 16), :]
                if a == 0:
                    side = first_row(side.astype(F32), jnp.zeros((1, WIDE), F32)).astype(BF16)
            else:
                side = jnp.zeros((16, WIDE), BF16)
            blocks.append(jnp.concatenate([xe[a * 3 + b], over, side], axis=0))
    rest = layer_one(blocks)
    ext[...] = gelu(rest[0:96] + bias1)
    above0 = ext[pl.ds(0, 32), :] * inside
    above1 = ext[pl.ds(32, 32), :] * inside
    hid1[0, pl.ds(0, 32), :] = above0.astype(BF16)
    hid1[1, pl.ds(0, 32), :] = above1.astype(BF16)
    hid1[2, pl.ds(0, 32), :] = down_one(above1, ext[pl.ds(80, 1), :] * inside).astype(BF16)
    side = rest[160:176]
    over = rest[96:160] + first_row(jnp.zeros((64, HID), F32), side[0:1])
    over = gelu(pre_top[...] + over)
    side = gelu(pre_left[...] + side)
    hid0[0, pl.ds(0, 32), :] = over[0:32].astype(BF16)
    hid0[1, pl.ds(0, 32), :] = over[32:64].astype(BF16)
    hid0[2, pl.ds(0, 32), :] = down_one(over[32:64], ext[pl.ds(64, 1), :]).astype(BF16)
    for ip in range(2):
        hid = hid1 if ip else hid0
        for i in range(8):
            n = ip * 8 + i
            if n == 0:
                continue
            at = pl.ds(i * 32 + (32 if ip else 0), 16)
            hid[0, at, :] = first_row(hid[0, at, :].astype(F32), side[n : n + 1]).astype(BF16)
            hid[2, at, :] = first_row(hid[2, at, :].astype(F32), ext[pl.ds(64 + n, 1), :]).astype(BF16)

    w2_copy.wait()
    pltpu.make_async_copy(obs.at[pl.ds(1, N - 1)], rows_in.at[pl.ds(1, N - 1)], send).wait()
    pltpu.make_async_copy(
        meta_out.at[0, pl.ds(1, N - 1)], meta_in.at[pl.ds(1, N - 1)], msend
    ).wait()


def layer_two(hid0, hid1, w2, b2, out):
    parts = []
    for a in range(3):
        for b in range(3):
            v = (2, 0, 1)[b]
            if a == 1:
                parts.append(hid0[v])
            else:
                parts.append(hid1[v, pl.ds(32 if a == 2 else 0, 256), :])
    second = jnp.dot(jnp.concatenate(parts, axis=1), w2[...], preferred_element_type=F32)
    out[...] = gelu(second + b2[...]).astype(BF16).reshape(8, 32, HID)


def on_device(obs, cells, counts, conv_in, conv_density, bias_in, conv_mid, bias_mid):
    vmem = pl.BlockSpec(memory_space=pltpu.VMEM)
    hbm = pl.BlockSpec(memory_space=pltpu.HBM)
    dma = pltpu.SemaphoreType.DMA
    hid0, hid1, w2 = pl.pallas_call(
        kernel,
        out_shape=[
            pltpu.VMEM((3, 256, HID), BF16),
            pltpu.VMEM((3, 288, HID), BF16),
            pltpu.VMEM((K2, HID), BF16),
        ],
        in_specs=[hbm] * 7,
        out_specs=[vmem, vmem, vmem],
        scratch_shapes=[
            pltpu.VMEM((SLOTS, N), jnp.int32),
            pltpu.VMEM((1, N), jnp.int32),
            pltpu.VMEM((3, 3, HID), F32),
            pltpu.VMEM((1, HID), F32),
            pltpu.VMEM((N, SLOTS, CH), BF16),
            pltpu.VMEM((4, N, 1, 128), jnp.int32),
            pltpu.VMEM((N, 1, 128), jnp.int32),
            pltpu.VMEM((4096, CH), F32),
            pltpu.VMEM((128, 128), F32),
            pltpu.VMEM((512, CH), F32),
            pltpu.VMEM((512, CH), BF16),
            pltpu.VMEM((32, 128), F32),
            pltpu.VMEM((384, 128), F32),
            pltpu.VMEM((16, 128), BF16),
            pltpu.VMEM((16, WIDE), F32),
            pltpu.VMEM((16, WIDE), BF16),
            pltpu.VMEM((384, CH), BF16),
            pltpu.VMEM((96, CH), BF16),
            pltpu.VMEM((16, WIDE), BF16),
            pltpu.VMEM((16, 128), BF16),
            pltpu.VMEM((16, 128), BF16),
            pltpu.VMEM((3, 1024, WIDE), BF16),
            pltpu.VMEM((3, 1088, WIDE), BF16),
            pltpu.VMEM((9, 96, WIDE), BF16),
            pltpu.VMEM((96, HID), F32),
            pltpu.VMEM((64, HID), F32),
            pltpu.VMEM((16, HID), F32),
            pltpu.VMEM((K1 + 128, HID), BF16),
            pltpu.VMEM((16, HID), F32),
            pltpu.SemaphoreType.REGULAR((4,)),
            dma,
            dma((GROUPS,)),
            dma,
            dma((GROUPS,)),
            dma((2,)),
            dma((4,)),
            dma((5,)),
            dma((5,)),
        ],
        compiler_params=pltpu.CompilerParams(
            collective_id=0, has_side_effects=True, vmem_limit_bytes=54 * 2**20
        ),
    )(
        obs,
        cells.T,
        counts.reshape(1, N),
        conv_in.reshape(K1, HID),
        conv_density,
        bias_in.reshape(1, HID),
        conv_mid.reshape(K2, HID),
    )
    return pl.pallas_call(
        layer_two,
        out_shape=jax.ShapeDtypeStruct((8, 32, HID), BF16),
        in_specs=[vmem, vmem, vmem, vmem],
        out_specs=vmem,
        compiler_params=pltpu.CompilerParams(vmem_limit_bytes=20 * 2**20),
    )(hid0, hid1, w2, bias_mid.reshape(1, HID))


def solution(mesh):
    return jax.shard_map(
        on_device,
        mesh=mesh,
        in_specs=(
            P(("lat", "lon"), None, None),
            P(("lat", "lon"), None),
            P(("lat", "lon")),
            P(),
            P(),
            P(),
            P(),
            P(),
        ),
        out_specs=P("lat", "lon", None),
        check_vma=False,
    )
```

```python
import functools

import jax
import jax.numpy as jnp
from jax import lax
from jax.experimental import pallas as pl
from jax.experimental.pallas import tpu as pltpu
from jax.sharding import PartitionSpec as P

MESH = pl.DeviceIdType.MESH
N = 128
SLOTS = 32
CH = 256
HID = 512
WIDE = CH + 128
PER = 8
GROUPS = N // PER
K1 = 9 * CH
K2 = 9 * HID
F32 = jnp.float32
BF16 = jnp.bfloat16


def position():
    lat = lax.axis_index("lat")
    lon = lax.axis_index("lon")
    return lon & 3, ((lat >> 1) << 1) + (lon >> 4), (lon >> 2) & 3, lat & 1


def around(v, d):
    return (v + d) & 3


def wrapped(v):
    return jnp.where(v > 2, v - 2, v + 1) if not isinstance(v, int) else v % 3 + 1


def gelu(x):
    return 0.5 * x * (1.0 + jnp.tanh(0.7978845608028654 * (x + 0.044715 * (x * x * x))))


def one_hot(ids, tag, want, height):
    if tag is not None:
        ids = jnp.where(tag == want, ids, jnp.full_like(ids, -1.0))
    rows = lax.broadcasted_iota(jnp.int32, (height, 128), 0).astype(F32).astype(BF16)
    rows = rows.reshape(height // 16, 16, 128)
    hit = rows == ids[None]
    return jnp.where(hit, jnp.ones_like(rows), jnp.zeros_like(rows)).reshape(height, 128)


def first_row(block, row):
    sub = lax.broadcasted_iota(jnp.int32, block.shape, 0)
    return jnp.where(sub == 0, jnp.broadcast_to(row, block.shape), block)


def down_one(block, row):
    return first_row(pltpu.roll(block, 1, 0), row)


def offset(q, ip, i):
    return ip * (576 if q else 512) + i * 64


def kernel(
    obs, cells_in, counts_in, w1, wd_in, b1_in, w2, hid0, hid1, w2v,
    cells, counts, wd, b1,
    rows_in, meta_out, meta_in, acc, dens, edge, edge_bf, edge_dens, edge_fr, edge_fr_bf, corner, corner_bf,
    top_in, left_in, corner_in, top_fr, left_fr,
    x0, x1, xe, ext, pre_top, pre_left, w1v, wdf,
    entered, send, recv, msend, mrecv, wsem, ssem, hsend, hrecv,
):
    small = [
        pltpu.make_async_copy(src, dst, ssem.at[i])
        for i, (src, dst) in enumerate(((cells_in, cells), (counts_in, counts), (wd_in, wd), (b1_in, b1)))
    ]
    for copy in small:
        copy.start()
    x_me, y_me, z_me, core_me = position()
    lat = lax.axis_index("lat")
    lon = lax.axis_index("lon")

    def device(dx, dy, dz, dc):
        y = around(y_me, dy)
        core = core_me ^ dc
        return (y & 2) + core, ((y & 1) << 4) + (around(z_me, dz) << 2) + around(x_me, dx)

    def signal(sem, offsets):
        for to in offsets:
            pl.semaphore_signal(sem, inc=1, device_id=device(*to), device_id_type=MESH)

    barrier = pltpu.get_barrier_semaphore()
    steps = (1, 2, 3)
    x_line = [(d, 0, 0, 0) for d in steps]
    y_line = [(0, d, 0, 0) for d in steps]
    z_line = [(0, 0, d, 0) for d in steps]
    lines = [(0, 0, 0, 1)] + [o[:3] + (c,) for o in x_line + y_line + z_line for c in (0, 1)]
    signal(barrier, lines)
    w1_copy = pltpu.make_async_copy(w1, w1v.at[pl.ds(0, K1)], wsem.at[0])
    w2_copy = pltpu.make_async_copy(w2, w2v, wsem.at[1])
    w2_copy.start()
    w1_copy.start()

    for copy in small:
        copy.wait()
    lane = lax.broadcasted_iota(jnp.int32, (N, 128), 1)
    slot = lax.broadcasted_iota(jnp.int32, (SLOTS, N), 0)
    coded = jnp.where(slot < counts[...], cells[...], -1)
    coded = jnp.transpose(jnp.concatenate([coded] * 4, axis=0))
    for v in range(4):
        meta_out[v] = jnp.where((lane >> 5) == v, coded, 0).reshape(N, 1, 128)

    @pl.when(lat == 0)
    def _():
        for ref in (top_in, corner_in, top_fr):
            ref[...] = jnp.zeros_like(ref)

    acc[...] = jnp.zeros_like(acc)
    dens[...] = jnp.zeros_like(dens)
    edge[...] = jnp.zeros_like(edge)
    edge_dens[...] = jnp.zeros_like(edge_dens)
    x1[:, pl.ds(512, 64), :] = jnp.zeros((3, 64, WIDE), BF16)
    wdf[...] = jnp.zeros_like(wdf)
    for a in range(3):
        wdf[3 * a : 3 * a + 3, :] = wd[a]
    taps = wdf[...]
    taps_hi = taps.astype(BF16)
    taps_lo = (taps - taps_hi.astype(F32)).astype(BF16)
    w1v[pl.ds(K1, 128), :] = jnp.concatenate(
        [taps_hi, taps_lo, jnp.zeros((96, HID), BF16)], axis=0
    )

    def dispatch(k, dx, dy, dz, dc):
        to_lat, to_lon = device(dx, dy, dz, dc)
        to = to_lat * 32 + to_lon
        src_meta, src = meta_out.at[k & 3, pl.ds(to, 1)], obs.at[pl.ds(to, 1)]
        dst_meta, dst = meta_in.at[pl.ds(k, 1)], rows_in.at[pl.ds(k, 1)]
        if isinstance(k, int) and k == 0:
            pltpu.make_async_copy(src_meta, dst_meta, mrecv.at[0]).start()
            pltpu.make_async_copy(src, dst, recv.at[0]).start()
            return
        to = (to_lat, to_lon)
        pltpu.make_async_remote_copy(
            src_ref=src_meta, dst_ref=dst_meta, send_sem=msend, recv_sem=mrecv.at[k >> 3],
            device_id=to, device_id_type=MESH,
        ).start()
        pltpu.make_async_remote_copy(
            src_ref=src, dst_ref=dst, send_sem=send, recv_sem=recv.at[k >> 3],
            device_id=to, device_id_type=MESH,
        ).start()

    pl.semaphore_wait(barrier, len(lines))
    signal(entered.at[0], y_line)
    signal(entered.at[1], z_line)
    signal(entered.at[2], z_line)
    dispatch(0, 0, 0, 0, 0)
    dispatch(1, 0, 0, 0, 1)

    def along_lines(b, carry):
        for axis in range(3):
            for dc in range(2):
                d = [0, 0, 0]
                d[axis] = b + 1
                dispatch(2 + b * 6 + axis * 2 + dc, *d, dc)
        return carry

    def along_planes(b, carry):
        for dc in range(2):
            for a in range(3):
                for plane in range(3):
                    d = [a + 1, wrapped(a + b)]
                    d.insert(2 - plane, 0)
                    dispatch(20 + b * 18 + a * 6 + plane * 2 + dc, *d, dc)
        return carry

    def elsewhere(b, carry):
        for dc in range(2):
            for c in range(3):
                for a in range(3):
                    dispatch(
                        74 + b * 18 + c * 6 + a * 2 + dc, a + 1, wrapped(a + b), wrapped(a + c), dc
                    )
        return carry

    lax.fori_loop(0, 3, along_lines, 0)
    pl.semaphore_wait(entered.at[0], 3)
    signal(entered.at[3], z_line)
    pl.semaphore_wait(entered.at[1], 3)
    pl.semaphore_wait(entered.at[2], 3)
    lax.fori_loop(0, 3, along_planes, 0)
    pl.semaphore_wait(entered.at[3], 3)
    lax.fori_loop(0, 3, elsewhere, 0)

    def spread(v):
        return jnp.broadcast_to(v.astype(F32), (16, 128)).astype(BF16)

    def codes(start, count):
        result = []
        for t in range(count // 4):
            cell = sum(meta_in[start + 4 * t + u] for u in range(4))
            alive = cell >= 0
            r = cell >> 7
            c = cell & 127
            col = (c & 1) * 64 + ((c >> 1) & 1) * 32 + (c >> 2)
            row = (r & 1) * 16 + ((r >> 1) & 1) * 8 + (r >> 2)
            pos = (
                (r & 1) * 2048 + (c & 1) * 1024 + ((r >> 1) & 1) * 512 + (r >> 2) * 64
                + ((c >> 1) & 1) * 32 + (c >> 2)
            )
            result.append(
                (
                    spread(pos & 255),
                    spread(jnp.where(alive, pos >> 8, 99)),
                    spread(pos & 127),
                    spread(jnp.where(alive, pos >> 7, 199)),
                    spread(col),
                    spread(jnp.where(alive, r - 29, 99)),
                    spread(jnp.where(alive & (c >= 125), (c - 125) * 32 + row, -1)),
                )
            )
        return result

    def across(code, which, tag, want, height):
        return jnp.concatenate(
            [one_hot(c[which], None if tag is None else c[tag], want, height) for c in code], axis=1
        )

    def dot_t(left, right):
        return lax.dot_general(left, right, (((1,), (1,)), ((), ())), preferred_element_type=F32)

    def gather_edges(code, block):
        rows = across(code, 5, None, None, 16)
        edge_dens[0:16, :] += dot_t(rows, across(code, 4, None, None, 128))
        last = across(code, 6, None, None, 128)
        edge_dens[16:32, :] += dot_t(jnp.ones_like(rows), last)
        for e in range(4):
            hot = across(code, 4, 5, e, 128) if e < 3 else last
            at = pl.ds(e * 128, 128)
            edge[at, :] += jnp.dot(hot, block, preferred_element_type=F32)

    def gather_cells(code, block):
        dens[...] += dot_t(across(code, 2, None, None, 128), across(code, 3, None, None, 128))
        for b in range(16):
            at = pl.ds(b * 256, 256)
            acc[at, :] += jnp.dot(across(code, 0, 1, b, 256), block, preferred_element_type=F32)

    def arrived(g, size):
        start = g * PER
        for u in range(size):
            one = pl.ds(start + u * PER, PER)
            pltpu.make_async_copy(meta_out.at[0, one], meta_in.at[one], mrecv.at[g + u]).wait()
            pltpu.make_async_copy(obs.at[one], rows_in.at[one], recv.at[g + u]).wait()
        count = size * PER
        return codes(start, count), rows_in[pl.ds(start, count)].reshape(count * SLOTS, CH)

    def group(g, carry):
        code, block = arrived(g * 2, 2)
        gather_edges(code, block)
        gather_cells(code, block)
        return carry

    lax.fori_loop(0, GROUPS // 2 - 1, group, 0)
    code, block = arrived(GROUPS - 2, 1)
    gather_edges(code, block)
    gather_cells(code, block)
    code, block = arrived(GROUPS - 1, 1)
    gather_edges(code, block)

    sub16 = lax.broadcasted_iota(jnp.int32, (16, 128), 0)
    amount = jnp.where(sub16 == 3, edge_dens[16:32, :], edge_dens[0:16, :])
    edge_fr_bf[...] = (amount / (1.0 + amount)).astype(BF16)
    amount = jnp.transpose(jnp.concatenate([amount, jnp.zeros((112, 128), F32)], axis=0))
    scales = 1.0 / jnp.maximum(amount, 1.0)
    fractions = amount / (1.0 + amount)
    for e in range(4):
        scale = jnp.broadcast_to(scales[:, e : e + 1], (128, 128))
        at = pl.ds(e * 128, 128)
        sums = edge[at, :]
        value = jnp.concatenate([sums[:, 0:128] * scale, sums[:, 128:CH] * scale], axis=1)
        edge[at, :] = value
        edge_bf[at, :] = value.astype(BF16)
        if e < 3:
            edge_fr[at, :] = jnp.broadcast_to(fractions[:, e : e + 1], (128, 128))
    corner[...] = jnp.zeros_like(corner)
    for a in range(3):
        for b, at in enumerate((95, 63, 127)):
            corner[pl.ds(a * 3 + b, 1), 0:CH] = edge[pl.ds(a * 128 + at, 1), :]
            corner[pl.ds(a * 3 + b, 1), CH:WIDE] = edge_fr[pl.ds(a * 128 + at, 1), :]
    corner_bf[...] = corner[...].astype(BF16)
    next_lat = (lat + 1) & 3
    next_lon = (lon + 1) & 31
    halos = [
        pltpu.make_async_remote_copy(
            src_ref=src, dst_ref=dst, send_sem=hsend.at[i], recv_sem=hrecv.at[i],
            device_id=to, device_id_type=MESH,
        )
        for i, (src, dst, to) in enumerate(
            (
                (edge_bf.at[pl.ds(0, 384)], top_in, (next_lat, lon)),
                (edge_bf.at[pl.ds(384, 96)], left_in, (lat, next_lon)),
                (corner_bf, corner_in, (next_lat, next_lon)),
                (edge_fr_bf, top_fr, (next_lat, lon)),
                (edge_fr_bf, left_fr, (lat, next_lon)),
            )
        )
    ]
    tops, lefts = (halos[0], halos[2], halos[3]), (halos[1], halos[4])
    for halo in lefts:
        halo.start()

    @pl.when(lat < 3)
    def _():
        for halo in tops:
            halo.start()

    gather_cells(code, block)

    count = dens[...]
    scale_all = 1.0 / jnp.maximum(count, 1.0)
    fraction_all = count / (1.0 + count)
    for h in range(32):
        scale = jnp.broadcast_to(scale_all[:, h : h + 1], (128, 128))
        fraction = jnp.broadcast_to(fraction_all[:, h : h + 1], (128, 128))
        sums = acc[pl.ds(h * 128, 128), :]
        value = jnp.concatenate([sums[:, 0:128] * scale, sums[:, 128:CH] * scale, fraction], axis=1)
        q, p, ip, i = h >> 4, (h >> 3) & 1, (h >> 2) & 1, (h & 3) * 2
        x = x1 if q else x0
        x[p, pl.ds(offset(q, ip, i), 128), :] = value.astype(BF16)
        if p:
            for half in range(2):
                part = value[half * 64 : half * 64 + 64]
                moved = jnp.concatenate([down_one(part[32:64], jnp.zeros((1, WIDE), F32)), part[0:32]], axis=0)
                x[2, pl.ds(offset(q, ip, i + half), 64), :] = moved.astype(BF16)

    w1_copy.wait()
    lanes = lax.broadcasted_iota(jnp.int32, (16, 128), 1)
    tap_of_lane = jnp.where(lanes < 32, lanes & 15, 99).astype(F32).astype(BF16)
    bias1 = b1[...]

    def layer_one(blocks):
        shares = jnp.zeros((blocks[0].shape[0] // 16, 16, 128), BF16)
        for t, data in enumerate(blocks):
            shares = jnp.where((tap_of_lane == t)[None], data[:, CH:].reshape(-1, 16, 128), shares)
        parts = [data[:, 0:CH] for data in blocks] + [shares.reshape(-1, 128)]
        return jnp.dot(jnp.concatenate(parts, axis=1), w1v[...], preferred_element_type=F32)

    for chunk in range(4):
        ip, half = chunk >> 1, chunk & 1
        blocks = []
        for a in range(3):
            for b in range(3):
                v = (2, 0, 1)[b]
                if a == 1:
                    x, at = x0, ip * 512 + half * 256
                elif a == 2:
                    x, at = x1, ip * 576 + half * 256
                else:
                    x, at = x1, (0 if ip else 512) + half * 256
                blocks.append(x[v, pl.ds(at, 256), :])
        first = layer_one(blocks) + bias1
        if chunk == 0:
            pre_top[...] = first[0:64]
        hidden = gelu(first)
        hid = hid1 if ip else hid0
        for k in range(4):
            i = half * 4 + k
            pre_left[pl.ds(ip * 8 + i, 1), :] = first[k * 64 : k * 64 + 1]
            at = pl.ds(i * 32 + (32 if ip else 0), 32)
            odd = hidden[k * 64 + 32 : k * 64 + 64]
            hid[0, at, :] = hidden[k * 64 : k * 64 + 32].astype(BF16)
            hid[1, at, :] = odd.astype(BF16)
            hid[2, at, :] = pltpu.roll(odd, 1, 0).astype(BF16)

    for halo in lefts:
        halo.wait()

    @pl.when(lat < 3)
    def _():
        for halo in tops:
            halo.wait_send()

    @pl.when(lat > 0)
    def _():
        for halo in tops:
            halo.wait_recv()

    inside = jnp.where(lat > 0, 1.0, 0.0).astype(F32)

    def columns(fr):
        return jnp.transpose(jnp.concatenate([fr[...].astype(F32), jnp.zeros((112, 128), F32)], axis=0))

    top_cols = columns(top_fr)
    left_cols = columns(left_fr)
    left = jnp.concatenate(
        [left_in[...].astype(F32), jnp.broadcast_to(left_cols[0:96, 3:4], (96, 128))], axis=1
    )
    diag = corner_in[...].astype(F32) * inside
    for a in range(3):
        rows = jnp.concatenate(
            [
                top_in[pl.ds(a * 128, 128), :].astype(F32),
                jnp.broadcast_to(top_cols[:, a : a + 1], (128, 128)),
            ],
            axis=1,
        ) * inside
        p0, p1 = rows[0:64], rows[64:128]
        moved = jnp.concatenate([down_one(p1[32:64], diag[a * 3 + 2 : a * 3 + 3]), p1[0:32]], axis=0)
        for b, top in enumerate((moved, p0, p1)):
            side = left[b * 32 : b * 32 + 32]
            if a == 0:
                side = jnp.concatenate([down_one(side[24:32], diag[6 + b : 7 + b]), side[16:24]], axis=0)
            else:
                side = side[(a - 1) * 16 : a * 16]
            angle = first_row(jnp.zeros((16, WIDE), F32), diag[a * 3 + b : a * 3 + b + 1])
            xe[a * 3 + b, pl.ds(0, 64), :] = top.astype(BF16)
            xe[a * 3 + b, pl.ds(64, 16), :] = side.astype(BF16)
            xe[a * 3 + b, pl.ds(80, 16), :] = angle.astype(BF16)
    blocks = []
    for a in range(3):
        for b in range(3):
            if a == 0:
                over = xe[6 + b, pl.ds(0, 64), :]
            else:
                over = jnp.zeros((64, WIDE), BF16)
            if b == 0:
                side = xe[a * 3 + 2, pl.ds(64, 16), :]
                if a == 0:
                    side = first_row(side.astype(F32), jnp.zeros((1, WIDE), F32)).astype(BF16)
            else:
                side = jnp.zeros((16, WIDE), BF16)
            blocks.append(jnp.concatenate([xe[a * 3 + b], over, side], axis=0))
    rest = layer_one(blocks)
    ext[...] = gelu(rest[0:96] + bias1)
    above0 = ext[pl.ds(0, 32), :] * inside
    above1 = ext[pl.ds(32, 32), :] * inside
    hid1[0, pl.ds(0, 32), :] = above0.astype(BF16)
    hid1[1, pl.ds(0, 32), :] = above1.astype(BF16)
    hid1[2, pl.ds(0, 32), :] = down_one(above1, ext[pl.ds(80, 1), :] * inside).astype(BF16)
    side = rest[160:176]
    over = rest[96:160] + first_row(jnp.zeros((64, HID), F32), side[0:1])
    over = gelu(pre_top[...] + over)
    side = gelu(pre_left[...] + side)
    hid0[0, pl.ds(0, 32), :] = over[0:32].astype(BF16)
    hid0[1, pl.ds(0, 32), :] = over[32:64].astype(BF16)
    hid0[2, pl.ds(0, 32), :] = down_one(over[32:64], ext[pl.ds(64, 1), :]).astype(BF16)
    for ip in range(2):
        hid = hid1 if ip else hid0
        for i in range(8):
            n = ip * 8 + i
            if n == 0:
                continue
            at = pl.ds(i * 32 + (32 if ip else 0), 16)
            hid[0, at, :] = first_row(hid[0, at, :].astype(F32), side[n : n + 1]).astype(BF16)
            hid[2, at, :] = first_row(hid[2, at, :].astype(F32), ext[pl.ds(64 + n, 1), :]).astype(BF16)

    w2_copy.wait()
    pltpu.make_async_copy(obs.at[pl.ds(1, N - 1)], rows_in.at[pl.ds(1, N - 1)], send).wait()
    pltpu.make_async_copy(
        meta_out.at[0, pl.ds(1, N - 1)], meta_in.at[pl.ds(1, N - 1)], msend
    ).wait()


def layer_two(hid0, hid1, w2, b2, out):
    parts = []
    for a in range(3):
        for b in range(3):
            v = (2, 0, 1)[b]
            if a == 1:
                parts.append(hid0[v])
            else:
                parts.append(hid1[v, pl.ds(32 if a == 2 else 0, 256), :])
    taps = jnp.concatenate(parts, axis=1)
    for n in range(2):
        at = pl.ds(n * 256, 256)
        second = jnp.dot(taps, w2[:, at], preferred_element_type=F32)
        out[:, :, at] = gelu(second + b2[:, at]).astype(BF16).reshape(8, 32, 256)


def on_device(obs, cells, counts, conv_in, conv_density, bias_in, conv_mid, bias_mid):
    vmem = pl.BlockSpec(memory_space=pltpu.VMEM)
    hbm = pl.BlockSpec(memory_space=pltpu.HBM)
    dma = pltpu.SemaphoreType.DMA
    hid0, hid1, w2 = pl.pallas_call(
        kernel,
        out_shape=[
            pltpu.VMEM((3, 256, HID), BF16),
            pltpu.VMEM((3, 288, HID), BF16),
            pltpu.VMEM((K2, HID), BF16),
        ],
        in_specs=[hbm] * 7,
        out_specs=[vmem, vmem, vmem],
        scratch_shapes=[
            pltpu.VMEM((SLOTS, N), jnp.int32),
            pltpu.VMEM((1, N), jnp.int32),
            pltpu.VMEM((3, 3, HID), F32),
            pltpu.VMEM((1, HID), F32),
            pltpu.VMEM((N, SLOTS, CH), BF16),
            pltpu.VMEM((4, N, 1, 128), jnp.int32),
            pltpu.VMEM((N, 1, 128), jnp.int32),
            pltpu.VMEM((4096, CH), F32),
            pltpu.VMEM((128, 128), F32),
            pltpu.VMEM((512, CH), F32),
            pltpu.VMEM((512, CH), BF16),
            pltpu.VMEM((32, 128), F32),
            pltpu.VMEM((384, 128), F32),
            pltpu.VMEM((16, 128), BF16),
            pltpu.VMEM((16, WIDE), F32),
            pltpu.VMEM((16, WIDE), BF16),
            pltpu.VMEM((384, CH), BF16),
            pltpu.VMEM((96, CH), BF16),
            pltpu.VMEM((16, WIDE), BF16),
            pltpu.VMEM((16, 128), BF16),
            pltpu.VMEM((16, 128), BF16),
            pltpu.VMEM((3, 1024, WIDE), BF16),
            pltpu.VMEM((3, 1088, WIDE), BF16),
            pltpu.VMEM((9, 96, WIDE), BF16),
            pltpu.VMEM((96, HID), F32),
            pltpu.VMEM((64, HID), F32),
            pltpu.VMEM((16, HID), F32),
            pltpu.VMEM((K1 + 128, HID), BF16),
            pltpu.VMEM((16, HID), F32),
            pltpu.SemaphoreType.REGULAR((4,)),
            dma,
            dma((GROUPS,)),
            dma,
            dma((GROUPS,)),
            dma((2,)),
            dma((4,)),
            dma((5,)),
            dma((5,)),
        ],
        compiler_params=pltpu.CompilerParams(
            collective_id=0, has_side_effects=True, vmem_limit_bytes=54 * 2**20
        ),
    )(
        obs,
        cells.T,
        counts.reshape(1, N),
        conv_in.reshape(K1, HID),
        conv_density,
        bias_in.reshape(1, HID),
        conv_mid.reshape(K2, HID),
    )
    return pl.pallas_call(
        layer_two,
        out_shape=jax.ShapeDtypeStruct((8, 32, HID), BF16),
        in_specs=[vmem, vmem, vmem, vmem],
        out_specs=vmem,
        compiler_params=pltpu.CompilerParams(vmem_limit_bytes=20 * 2**20),
    )(hid0, hid1, w2, bias_mid.reshape(1, HID))


def solution(mesh):
    return jax.shard_map(
        on_device,
        mesh=mesh,
        in_specs=(
            P(("lat", "lon"), None, None),
            P(("lat", "lon"), None),
            P(("lat", "lon")),
            P(),
            P(),
            P(),
            P(),
            P(),
        ),
        out_specs=P("lat", "lon", None),
        check_vma=False,
    )
```

```python
import functools

import jax
import jax.numpy as jnp
from jax import lax
from jax.experimental import pallas as pl
from jax.experimental.pallas import tpu as pltpu
from jax.sharding import PartitionSpec as P

MESH = pl.DeviceIdType.MESH
N = 128
SLOTS = 32
CH = 256
HID = 512
WIDE = CH + 128
PER = 8
GROUPS = N // PER
K1 = 9 * CH
K2 = 9 * HID
F32 = jnp.float32
BF16 = jnp.bfloat16


def position():
    lat = lax.axis_index("lat")
    lon = lax.axis_index("lon")
    return lon & 3, ((lat >> 1) << 1) + (lon >> 4), (lon >> 2) & 3, lat & 1


def around(v, d):
    return (v + d) & 3


def wrapped(v):
    return jnp.where(v > 2, v - 2, v + 1) if not isinstance(v, int) else v % 3 + 1


def gelu(x):
    return 0.5 * x * (1.0 + jnp.tanh(0.7978845608028654 * (x + 0.044715 * (x * x * x))))


def one_hot(ids, tag, want, height):
    if tag is not None:
        ids = jnp.where(tag == want, ids, jnp.full_like(ids, -1.0))
    rows = lax.broadcasted_iota(jnp.int32, (height, 128), 0).astype(F32).astype(BF16)
    rows = rows.reshape(height // 16, 16, 128)
    hit = rows == ids[None]
    return jnp.where(hit, jnp.ones_like(rows), jnp.zeros_like(rows)).reshape(height, 128)


def first_row(block, row):
    sub = lax.broadcasted_iota(jnp.int32, block.shape, 0)
    return jnp.where(sub == 0, jnp.broadcast_to(row, block.shape), block)


def down_one(block, row):
    return first_row(pltpu.roll(block, 1, 0), row)


def offset(q, ip, i):
    return ip * (576 if q else 512) + i * 64


def kernel(
    obs, cells_in, counts_in, w1, wd_in, b1_in, w2, hid0, hid1, w2v,
    cells, counts, wd, b1,
    rows_in, meta_out, meta_in, acc, dens, edge, edge_bf, edge_dens, edge_fr, edge_fr_bf, corner, corner_bf,
    top_in, left_in, corner_in, top_fr, left_fr,
    x0, x1, xe, ext, pre_top, pre_left, w1v, wdf,
    entered, send, recv, msend, mrecv, wsem, ssem, hsend, hrecv,
):
    small = [
        pltpu.make_async_copy(src, dst, ssem.at[i])
        for i, (src, dst) in enumerate(((cells_in, cells), (counts_in, counts), (wd_in, wd), (b1_in, b1)))
    ]
    for copy in small:
        copy.start()
    x_me, y_me, z_me, core_me = position()
    lat = lax.axis_index("lat")
    lon = lax.axis_index("lon")

    def device(dx, dy, dz, dc):
        y = around(y_me, dy)
        core = core_me ^ dc
        return (y & 2) + core, ((y & 1) << 4) + (around(z_me, dz) << 2) + around(x_me, dx)

    def signal(sem, offsets):
        for to in offsets:
            pl.semaphore_signal(sem, inc=1, device_id=device(*to), device_id_type=MESH)

    barrier = pltpu.get_barrier_semaphore()
    steps = (1, 2, 3)
    x_line = [(d, 0, 0, 0) for d in steps]
    y_line = [(0, d, 0, 0) for d in steps]
    z_line = [(0, 0, d, 0) for d in steps]
    lines = [(0, 0, 0, 1)] + [o[:3] + (c,) for o in x_line + y_line + z_line for c in (0, 1)]
    signal(barrier, lines)
    w1_copy = pltpu.make_async_copy(w1, w1v.at[pl.ds(0, K1)], wsem.at[0])
    w2_copy = pltpu.make_async_copy(w2, w2v, wsem.at[1])
    w2_copy.start()
    w1_copy.start()

    for copy in small:
        copy.wait()
    lane = lax.broadcasted_iota(jnp.int32, (N, 128), 1)
    slot = lax.broadcasted_iota(jnp.int32, (SLOTS, N), 0)
    coded = jnp.where(slot < counts[...], cells[...], -1)
    coded = jnp.transpose(jnp.concatenate([coded] * 4, axis=0))
    for v in range(4):
        meta_out[v] = jnp.where((lane >> 5) == v, coded, 0).reshape(N, 1, 128)

    def dispatch(k, dx, dy, dz, dc):
        to_lat, to_lon = device(dx, dy, dz, dc)
        to = to_lat * 32 + to_lon
        src_meta, src = meta_out.at[k & 3, pl.ds(to, 1)], obs.at[pl.ds(to, 1)]
        dst_meta, dst = meta_in.at[pl.ds(k, 1)], rows_in.at[pl.ds(k, 1)]
        if isinstance(k, int) and k == 0:
            pltpu.make_async_copy(src_meta, dst_meta, mrecv.at[0]).start()
            pltpu.make_async_copy(src, dst, recv.at[0]).start()
            return
        to = (to_lat, to_lon)
        pltpu.make_async_remote_copy(
            src_ref=src_meta, dst_ref=dst_meta, send_sem=msend, recv_sem=mrecv.at[k >> 3],
            device_id=to, device_id_type=MESH,
        ).start()
        pltpu.make_async_remote_copy(
            src_ref=src, dst_ref=dst, send_sem=send, recv_sem=recv.at[k >> 3],
            device_id=to, device_id_type=MESH,
        ).start()

    pl.semaphore_wait(barrier, len(lines))
    signal(entered.at[0], y_line)
    signal(entered.at[1], z_line)
    signal(entered.at[2], z_line)
    dispatch(0, 0, 0, 0, 0)
    dispatch(1, 0, 0, 0, 1)

    def along_lines(b, carry):
        for axis in range(3):
            for dc in range(2):
                d = [0, 0, 0]
                d[axis] = b + 1
                dispatch(2 + b * 6 + axis * 2 + dc, *d, dc)
        return carry

    def along_planes(b, carry):
        for dc in range(2):
            for a in range(3):
                for plane in range(3):
                    d = [a + 1, wrapped(a + b)]
                    d.insert(2 - plane, 0)
                    dispatch(20 + b * 18 + a * 6 + plane * 2 + dc, *d, dc)
        return carry

    def elsewhere(b, carry):
        for dc in range(2):
            for c in range(3):
                for a in range(3):
                    dispatch(
                        74 + b * 18 + c * 6 + a * 2 + dc, a + 1, wrapped(a + b), wrapped(a + c), dc
                    )
        return carry

    lax.fori_loop(0, 3, along_lines, 0)
    pl.semaphore_wait(entered.at[0], 3)
    signal(entered.at[3], z_line)
    pl.semaphore_wait(entered.at[1], 3)
    pl.semaphore_wait(entered.at[2], 3)
    lax.fori_loop(0, 3, along_planes, 0)
    pl.semaphore_wait(entered.at[3], 3)
    lax.fori_loop(0, 3, elsewhere, 0)

    @pl.when(lat == 0)
    def _():
        for ref in (top_in, corner_in, top_fr):
            ref[...] = jnp.zeros_like(ref)

    acc[...] = jnp.zeros_like(acc)
    dens[...] = jnp.zeros_like(dens)
    edge[...] = jnp.zeros_like(edge)
    edge_dens[...] = jnp.zeros_like(edge_dens)
    x1[:, pl.ds(512, 64), :] = jnp.zeros((3, 64, WIDE), BF16)
    wdf[...] = jnp.zeros_like(wdf)
    for a in range(3):
        wdf[3 * a : 3 * a + 3, :] = wd[a]
    taps = wdf[...]
    taps_hi = taps.astype(BF16)
    taps_lo = (taps - taps_hi.astype(F32)).astype(BF16)
    w1v[pl.ds(K1, 128), :] = jnp.concatenate(
        [taps_hi, taps_lo, jnp.zeros((96, HID), BF16)], axis=0
    )

    def spread(v):
        return jnp.broadcast_to(v.astype(F32), (16, 128)).astype(BF16)

    def codes(start, count):
        result = []
        for t in range(count // 4):
            cell = sum(meta_in[start + 4 * t + u] for u in range(4))
            alive = cell >= 0
            r = cell >> 7
            c = cell & 127
            col = (c & 1) * 64 + ((c >> 1) & 1) * 32 + (c >> 2)
            row = (r & 1) * 16 + ((r >> 1) & 1) * 8 + (r >> 2)
            pos = (
                (r & 1) * 2048 + (c & 1) * 1024 + ((r >> 1) & 1) * 512 + (r >> 2) * 64
                + ((c >> 1) & 1) * 32 + (c >> 2)
            )
            result.append(
                (
                    spread(pos & 255),
                    spread(jnp.where(alive, pos >> 8, 99)),
                    spread(pos & 127),
                    spread(jnp.where(alive, pos >> 7, 199)),
                    spread(col),
                    spread(jnp.where(alive, r - 29, 99)),
                    spread(jnp.where(alive & (c >= 125), (c - 125) * 32 + row, -1)),
                )
            )
        return result

    def across(code, which, tag, want, height):
        return jnp.concatenate(
            [one_hot(c[which], None if tag is None else c[tag], want, height) for c in code], axis=1
        )

    def dot_t(left, right):
        return lax.dot_general(left, right, (((1,), (1,)), ((), ())), preferred_element_type=F32)

    def gather_edges(code, block):
        rows = across(code, 5, None, None, 16)
        edge_dens[0:16, :] += dot_t(rows, across(code, 4, None, None, 128))
        last = across(code, 6, None, None, 128)
        edge_dens[16:32, :] += dot_t(jnp.ones_like(rows), last)
        for e in range(4):
            hot = across(code, 4, 5, e, 128) if e < 3 else last
            at = pl.ds(e * 128, 128)
            edge[at, :] += jnp.dot(hot, block, preferred_element_type=F32)

    def gather_cells(code, block):
        dens[...] += dot_t(across(code, 2, None, None, 128), across(code, 3, None, None, 128))
        for b in range(16):
            at = pl.ds(b * 256, 256)
            acc[at, :] += jnp.dot(across(code, 0, 1, b, 256), block, preferred_element_type=F32)

    def arrived(g, size):
        start = g * PER
        for u in range(size):
            one = pl.ds(start + u * PER, PER)
            pltpu.make_async_copy(meta_out.at[0, one], meta_in.at[one], mrecv.at[g + u]).wait()
            pltpu.make_async_copy(obs.at[one], rows_in.at[one], recv.at[g + u]).wait()
        count = size * PER
        return codes(start, count), rows_in[pl.ds(start, count)].reshape(count * SLOTS, CH)

    def group(g, carry):
        code, block = arrived(g * 2, 2)
        gather_edges(code, block)
        gather_cells(code, block)
        return carry

    lax.fori_loop(0, GROUPS // 2 - 1, group, 0)
    code, block = arrived(GROUPS - 2, 1)
    gather_edges(code, block)
    gather_cells(code, block)
    code, block = arrived(GROUPS - 1, 1)
    gather_edges(code, block)

    sub16 = lax.broadcasted_iota(jnp.int32, (16, 128), 0)
    amount = jnp.where(sub16 == 3, edge_dens[16:32, :], edge_dens[0:16, :])
    edge_fr_bf[...] = (amount / (1.0 + amount)).astype(BF16)
    amount = jnp.transpose(jnp.concatenate([amount, jnp.zeros((112, 128), F32)], axis=0))
    scales = 1.0 / jnp.maximum(amount, 1.0)
    fractions = amount / (1.0 + amount)
    for e in range(4):
        scale = jnp.broadcast_to(scales[:, e : e + 1], (128, 128))
        at = pl.ds(e * 128, 128)
        sums = edge[at, :]
        value = jnp.concatenate([sums[:, 0:128] * scale, sums[:, 128:CH] * scale], axis=1)
        edge[at, :] = value
        edge_bf[at, :] = value.astype(BF16)
        if e < 3:
            edge_fr[at, :] = jnp.broadcast_to(fractions[:, e : e + 1], (128, 128))
    corner[...] = jnp.zeros_like(corner)
    for a in range(3):
        for b, at in enumerate((95, 63, 127)):
            corner[pl.ds(a * 3 + b, 1), 0:CH] = edge[pl.ds(a * 128 + at, 1), :]
            corner[pl.ds(a * 3 + b, 1), CH:WIDE] = edge_fr[pl.ds(a * 128 + at, 1), :]
    corner_bf[...] = corner[...].astype(BF16)
    next_lat = (lat + 1) & 3
    next_lon = (lon + 1) & 31
    halos = [
        pltpu.make_async_remote_copy(
            src_ref=src, dst_ref=dst, send_sem=hsend.at[i], recv_sem=hrecv.at[i],
            device_id=to, device_id_type=MESH,
        )
        for i, (src, dst, to) in enumerate(
            (
                (edge_bf.at[pl.ds(0, 384)], top_in, (next_lat, lon)),
                (edge_bf.at[pl.ds(384, 96)], left_in, (lat, next_lon)),
                (corner_bf, corner_in, (next_lat, next_lon)),
                (edge_fr_bf, top_fr, (next_lat, lon)),
                (edge_fr_bf, left_fr, (lat, next_lon)),
            )
        )
    ]
    tops, lefts = (halos[0], halos[2], halos[3]), (halos[1], halos[4])
    for halo in lefts:
        halo.start()

    @pl.when(lat < 3)
    def _():
        for halo in tops:
            halo.start()

    gather_cells(code, block)

    count = dens[...]
    scale_all = 1.0 / jnp.maximum(count, 1.0)
    fraction_all = count / (1.0 + count)
    for h in range(32):
        scale = jnp.broadcast_to(scale_all[:, h : h + 1], (128, 128))
        fraction = jnp.broadcast_to(fraction_all[:, h : h + 1], (128, 128))
        sums = acc[pl.ds(h * 128, 128), :]
        value = jnp.concatenate([sums[:, 0:128] * scale, sums[:, 128:CH] * scale, fraction], axis=1)
        q, p, ip, i = h >> 4, (h >> 3) & 1, (h >> 2) & 1, (h & 3) * 2
        x = x1 if q else x0
        x[p, pl.ds(offset(q, ip, i), 128), :] = value.astype(BF16)
        if p:
            for half in range(2):
                part = value[half * 64 : half * 64 + 64]
                moved = jnp.concatenate([down_one(part[32:64], jnp.zeros((1, WIDE), F32)), part[0:32]], axis=0)
                x[2, pl.ds(offset(q, ip, i + half), 64), :] = moved.astype(BF16)

    w1_copy.wait()
    lanes = lax.broadcasted_iota(jnp.int32, (16, 128), 1)
    tap_of_lane = jnp.where(lanes < 32, lanes & 15, 99).astype(F32).astype(BF16)
    bias1 = b1[...]

    def layer_one(blocks):
        shares = jnp.zeros((blocks[0].shape[0] // 16, 16, 128), BF16)
        for t, data in enumerate(blocks):
            shares = jnp.where((tap_of_lane == t)[None], data[:, CH:].reshape(-1, 16, 128), shares)
        parts = [data[:, 0:CH] for data in blocks] + [shares.reshape(-1, 128)]
        return jnp.dot(jnp.concatenate(parts, axis=1), w1v[...], preferred_element_type=F32)

    for chunk in range(4):
        ip, half = chunk >> 1, chunk & 1
        blocks = []
        for a in range(3):
            for b in range(3):
                v = (2, 0, 1)[b]
                if a == 1:
                    x, at = x0, ip * 512 + half * 256
                elif a == 2:
                    x, at = x1, ip * 576 + half * 256
                else:
                    x, at = x1, (0 if ip else 512) + half * 256
                blocks.append(x[v, pl.ds(at, 256), :])
        first = layer_one(blocks) + bias1
        if chunk == 0:
            pre_top[...] = first[0:64]
        hidden = gelu(first)
        hid = hid1 if ip else hid0
        for k in range(4):
            i = half * 4 + k
            pre_left[pl.ds(ip * 8 + i, 1), :] = first[k * 64 : k * 64 + 1]
            at = pl.ds(i * 32 + (32 if ip else 0), 32)
            odd = hidden[k * 64 + 32 : k * 64 + 64]
            hid[0, at, :] = hidden[k * 64 : k * 64 + 32].astype(BF16)
            hid[1, at, :] = odd.astype(BF16)
            hid[2, at, :] = pltpu.roll(odd, 1, 0).astype(BF16)

    for halo in lefts:
        halo.wait()

    @pl.when(lat < 3)
    def _():
        for halo in tops:
            halo.wait_send()

    @pl.when(lat > 0)
    def _():
        for halo in tops:
            halo.wait_recv()

    inside = jnp.where(lat > 0, 1.0, 0.0).astype(F32)

    def columns(fr):
        return jnp.transpose(jnp.concatenate([fr[...].astype(F32), jnp.zeros((112, 128), F32)], axis=0))

    top_cols = columns(top_fr)
    left_cols = columns(left_fr)
    left = jnp.concatenate(
        [left_in[...].astype(F32), jnp.broadcast_to(left_cols[0:96, 3:4], (96, 128))], axis=1
    )
    diag = corner_in[...].astype(F32) * inside
    for a in range(3):
        rows = jnp.concatenate(
            [
                top_in[pl.ds(a * 128, 128), :].astype(F32),
                jnp.broadcast_to(top_cols[:, a : a + 1], (128, 128)),
            ],
            axis=1,
        ) * inside
        p0, p1 = rows[0:64], rows[64:128]
        moved = jnp.concatenate([down_one(p1[32:64], diag[a * 3 + 2 : a * 3 + 3]), p1[0:32]], axis=0)
        for b, top in enumerate((moved, p0, p1)):
            side = left[b * 32 : b * 32 + 32]
            if a == 0:
                side = jnp.concatenate([down_one(side[24:32], diag[6 + b : 7 + b]), side[16:24]], axis=0)
            else:
                side = side[(a - 1) * 16 : a * 16]
            angle = first_row(jnp.zeros((16, WIDE), F32), diag[a * 3 + b : a * 3 + b + 1])
            xe[a * 3 + b, pl.ds(0, 64), :] = top.astype(BF16)
            xe[a * 3 + b, pl.ds(64, 16), :] = side.astype(BF16)
            xe[a * 3 + b, pl.ds(80, 16), :] = angle.astype(BF16)
    blocks = []
    for a in range(3):
        for b in range(3):
            if a == 0:
                over = xe[6 + b, pl.ds(0, 64), :]
            else:
                over = jnp.zeros((64, WIDE), BF16)
            if b == 0:
                side = xe[a * 3 + 2, pl.ds(64, 16), :]
                if a == 0:
                    side = first_row(side.astype(F32), jnp.zeros((1, WIDE), F32)).astype(BF16)
            else:
                side = jnp.zeros((16, WIDE), BF16)
            blocks.append(jnp.concatenate([xe[a * 3 + b], over, side], axis=0))
    rest = layer_one(blocks)
    ext[...] = gelu(rest[0:96] + bias1)
    above0 = ext[pl.ds(0, 32), :] * inside
    above1 = ext[pl.ds(32, 32), :] * inside
    hid1[0, pl.ds(0, 32), :] = above0.astype(BF16)
    hid1[1, pl.ds(0, 32), :] = above1.astype(BF16)
    hid1[2, pl.ds(0, 32), :] = down_one(above1, ext[pl.ds(80, 1), :] * inside).astype(BF16)
    side = rest[160:176]
    over = rest[96:160] + first_row(jnp.zeros((64, HID), F32), side[0:1])
    over = gelu(pre_top[...] + over)
    side = gelu(pre_left[...] + side)
    hid0[0, pl.ds(0, 32), :] = over[0:32].astype(BF16)
    hid0[1, pl.ds(0, 32), :] = over[32:64].astype(BF16)
    hid0[2, pl.ds(0, 32), :] = down_one(over[32:64], ext[pl.ds(64, 1), :]).astype(BF16)
    for ip in range(2):
        hid = hid1 if ip else hid0
        for i in range(8):
            n = ip * 8 + i
            if n == 0:
                continue
            at = pl.ds(i * 32 + (32 if ip else 0), 16)
            hid[0, at, :] = first_row(hid[0, at, :].astype(F32), side[n : n + 1]).astype(BF16)
            hid[2, at, :] = first_row(hid[2, at, :].astype(F32), ext[pl.ds(64 + n, 1), :]).astype(BF16)

    w2_copy.wait()
    pltpu.make_async_copy(obs.at[pl.ds(1, N - 1)], rows_in.at[pl.ds(1, N - 1)], send).wait()
    pltpu.make_async_copy(
        meta_out.at[0, pl.ds(1, N - 1)], meta_in.at[pl.ds(1, N - 1)], msend
    ).wait()


def layer_two(hid0, hid1, w2, b2, out):
    parts = []
    for a in range(3):
        for b in range(3):
            v = (2, 0, 1)[b]
            if a == 1:
                parts.append(hid0[v])
            else:
                parts.append(hid1[v, pl.ds(32 if a == 2 else 0, 256), :])
    second = jnp.dot(jnp.concatenate(parts, axis=1), w2[...], preferred_element_type=F32)
    out[...] = gelu(second + b2[...]).astype(BF16).reshape(8, 32, HID)


def on_device(obs, cells, counts, conv_in, conv_density, bias_in, conv_mid, bias_mid):
    vmem = pl.BlockSpec(memory_space=pltpu.VMEM)
    hbm = pl.BlockSpec(memory_space=pltpu.HBM)
    dma = pltpu.SemaphoreType.DMA
    hid0, hid1, w2 = pl.pallas_call(
        kernel,
        out_shape=[
            pltpu.VMEM((3, 256, HID), BF16),
            pltpu.VMEM((3, 288, HID), BF16),
            pltpu.VMEM((K2, HID), BF16),
        ],
        in_specs=[hbm] * 7,
        out_specs=[vmem, vmem, vmem],
        scratch_shapes=[
            pltpu.VMEM((SLOTS, N), jnp.int32),
            pltpu.VMEM((1, N), jnp.int32),
            pltpu.VMEM((3, 3, HID), F32),
            pltpu.VMEM((1, HID), F32),
            pltpu.VMEM((N, SLOTS, CH), BF16),
            pltpu.VMEM((4, N, 1, 128), jnp.int32),
            pltpu.VMEM((N, 1, 128), jnp.int32),
            pltpu.VMEM((4096, CH), F32),
            pltpu.VMEM((128, 128), F32),
            pltpu.VMEM((512, CH), F32),
            pltpu.VMEM((512, CH), BF16),
            pltpu.VMEM((32, 128), F32),
            pltpu.VMEM((384, 128), F32),
            pltpu.VMEM((16, 128), BF16),
            pltpu.VMEM((16, WIDE), F32),
            pltpu.VMEM((16, WIDE), BF16),
            pltpu.VMEM((384, CH), BF16),
            pltpu.VMEM((96, CH), BF16),
            pltpu.VMEM((16, WIDE), BF16),
            pltpu.VMEM((16, 128), BF16),
            pltpu.VMEM((16, 128), BF16),
            pltpu.VMEM((3, 1024, WIDE), BF16),
            pltpu.VMEM((3, 1088, WIDE), BF16),
            pltpu.VMEM((9, 96, WIDE), BF16),
            pltpu.VMEM((96, HID), F32),
            pltpu.VMEM((64, HID), F32),
            pltpu.VMEM((16, HID), F32),
            pltpu.VMEM((K1 + 128, HID), BF16),
            pltpu.VMEM((16, HID), F32),
            pltpu.SemaphoreType.REGULAR((4,)),
            dma,
            dma((GROUPS,)),
            dma,
            dma((GROUPS,)),
            dma((2,)),
            dma((4,)),
            dma((5,)),
            dma((5,)),
        ],
        compiler_params=pltpu.CompilerParams(
            collective_id=0, has_side_effects=True, vmem_limit_bytes=54 * 2**20
        ),
    )(
        obs,
        cells.T,
        counts.reshape(1, N),
        conv_in.reshape(K1, HID),
        conv_density,
        bias_in.reshape(1, HID),
        conv_mid.reshape(K2, HID),
    )
    return pl.pallas_call(
        layer_two,
        out_shape=jax.ShapeDtypeStruct((8, 32, HID), BF16),
        in_specs=[vmem, vmem, vmem, vmem],
        out_specs=vmem,
        compiler_params=pltpu.CompilerParams(vmem_limit_bytes=20 * 2**20),
    )(hid0, hid1, w2, bias_mid.reshape(1, HID))


def solution(mesh):
    return jax.shard_map(
        on_device,
        mesh=mesh,
        in_specs=(
            P(("lat", "lon"), None, None),
            P(("lat", "lon"), None),
            P(("lat", "lon")),
            P(),
            P(),
            P(),
            P(),
            P(),
        ),
        out_specs=P("lat", "lon", None),
        check_vma=False,
    )
```
